32 devices in a mesh: store: 8 (over y, x, core), ctx: 4 (over z).
Axes of the slice: x: 2, y: 2, z: 4, core: 2. Of those that a mesh axis runs over, the one named last changes fastest.
Arguments:
- store_kv: bfloat16 [256, 32, 1024], P('store', 'ctx'), may hold values from -136 to 136, as said below
- block_slot: int32 [8, 16], P('store'), may hold values from 0 to 31, as said below
- block_owner: int32 [8, 16], P('store'), may hold values from 0 to 7, as said below
- rec_pos: int32 [8, 256], P('store'), may hold values from 0 to 511, as said below
- states: bfloat16 [8, 256, 8192], P('store', 'ctx'), may hold values from -6 to 6
- w_query: bfloat16 [8192, 4096], P('store', 'ctx'), may hold values from -0.0625 to 0.0625
- w_keyval: bfloat16 [8192, 1024], P('store', 'ctx'), may hold values from -0.125 to 0.125
Outputs:
- attended: bfloat16 [8, 256, 4096], P('store', None, 'ctx')
The draws below stay inside these ranges and needn't reach their ends.
Inputs may be any that keep to these rules, and one draw needn't show every extreme that they name: store_kv entries lie within the stated bounds. `block_slot`: ids are distinct within a request. `block_owner`: no owner appears more than 2 times in one request's list, and in every list some owner appears exactly 2 times. `rec_pos`: positions are distinct within a request and include 0 and 511.
All inputs are finite; a program needn't handle non-finite values.
Results may differ from the reference program's by a relative error of at most 0.0033.
The reference program's roundings to bfloat16 on the way (of `blocks`, `normed`, `queries`, `fresh`, `fresh_key`, `assembled` and `weights`) count: a program that leaves them out, or rounds other values in their place, can miss the bound.
Values may be sent and summed in bfloat16 or wider, within the bound.
No kernel may reach another device: no remote copies, remote signals or barrier semaphores. Data moves between devices by JAX's collectives and lax.ppermute only.
A program may use at most 128 MiB of HBM per device.

```python
import math
import jax
import jax.numpy as jnp
from jax import lax

D = 8192
QH = 32
KVH = 4
HD = 128
PIECE = 8
NB = 16
SB = 32
CAP = 2
REC = 256
CTX = 512
KVD = 1024
N_STORE = 8
N_CTX = 4


def draw_store_kv(key, part):
    key = jax.random.fold_in(key, 11)
    base_key = jax.random.fold_in(key, 0)
    shape = (N_STORE * SB, PIECE * N_CTX, 2 * KVH * HD)
    values = 2.0 * jax.random.truncated_normal(base_key, -6.0, 6.0, shape, jnp.float32)
    return values.astype(jnp.bfloat16)


def draw_block_slot(key, part):
    key = jax.random.fold_in(key, 3)
    row_keys = jax.random.split(key, 2 * N_STORE)
    inner = jax.vmap(lambda row_key: jax.random.permutation(row_key, SB - 2)[:NB - 2] + 1)(row_keys[:N_STORE])
    ends = jnp.broadcast_to(jnp.array([0, SB - 1], jnp.int32), (N_STORE, 2))
    joined = jnp.concatenate((ends, inner.astype(jnp.int32)), axis=1)
    shuffles = jax.vmap(lambda row_key: jax.random.permutation(row_key, NB))(row_keys[N_STORE:])
    return jnp.take_along_axis(joined, shuffles, axis=1).astype(jnp.int32)


def draw_block_owner(key, part):
    key = jax.random.fold_in(key, 5)
    heat_key, noise_key, order_key = jax.random.split(key, 3)
    storage_pool_size = CAP * N_STORE
    table_entries = jnp.arange(storage_pool_size, dtype=jnp.int32)
    owning_document = table_entries % N_STORE
    popularity = jax.random.permutation(heat_key, N_STORE).astype(jnp.int32)
    reward_boost = jnp.where(popularity == N_STORE - 1, 4 * N_STORE, 0).astype(jnp.int32)
    first_row = (jnp.arange(N_STORE) == 0)[:, None]
    ends = ((owning_document == 0) | (owning_document == N_STORE - 1))[None, :]
    surplus_amount = jnp.where(first_row & ends, 4 * N_STORE, 0).astype(jnp.int32)
    random_jitter = jax.random.randint(noise_key, (N_STORE, storage_pool_size), 0, N_STORE).astype(jnp.int32)
    ranking_score = (random_jitter + popularity[owning_document][None, :] + reward_boost[owning_document][None, :] + surplus_amount) * storage_pool_size + table_entries[None, :]
    picked = lax.top_k(ranking_score, NB)[1]
    shuffles = jax.vmap(lambda row_key: jax.random.permutation(row_key, NB))(jax.random.split(order_key, N_STORE))
    chosen = jnp.take_along_axis(picked, shuffles, axis=1)
    return (chosen % N_STORE).astype(jnp.int32)


def draw_rec_pos(key, part):
    key = jax.random.fold_in(key, 9)
    row_keys = jax.random.split(key, 2 * N_STORE)
    inner = jax.vmap(lambda row_key: jax.random.permutation(row_key, CTX - 2)[:REC - 2] + 1)(row_keys[:N_STORE])
    ends = jnp.broadcast_to(jnp.array([0, CTX - 1], jnp.int32), (N_STORE, 2))
    joined = jnp.concatenate((ends, inner.astype(jnp.int32)), axis=1)
    shuffles = jax.vmap(lambda row_key: jax.random.permutation(row_key, REC))(row_keys[N_STORE:])
    return jnp.take_along_axis(joined, shuffles, axis=1).astype(jnp.int32)


def block_scale(own_key, shape, shards, least, high):
    level, own = 1.0, jax.random.fold_in(own_key, 6)
    for position, shards_of in shards:
        draws = jnp.exp(jax.random.uniform(jax.random.fold_in(own, position), (shards_of,), jnp.float32, least / len(shards), high / len(shards)))
        level = level * jnp.repeat(draws, shape[position] // shards_of).reshape([-1 if axis == position else 1 for axis in range(len(shape))])
    return level


def gaussian(key, dims, deviation, limit, shards=(), kind=jnp.bfloat16):
    factor_of = block_scale(key, dims, shards, -0.22, 0.18) if shards else 1.0
    entries = jax.random.normal(key, dims, jnp.float32) * deviation * factor_of
    return jnp.minimum(jnp.maximum(entries, -limit), limit).astype(kind)


def setup_inputs(seed: int = 0) -> dict:
    splits = jax.random.split(jax.random.key(seed), 8)
    return {
        "store_kv": draw_store_kv(jax.random.fold_in(splits[7], 71), 0),
        "block_slot": draw_block_slot(jax.random.fold_in(splits[7], 71), 0),
        "block_owner": draw_block_owner(jax.random.fold_in(splits[7], 71), 0),
        "rec_pos": draw_rec_pos(jax.random.fold_in(splits[7], 71), 0),
        "states": gaussian(splits[4], (N_STORE, REC, D), 1.0, 6.0, ((0, 8), (1, 4))),
        "w_query": gaussian(splits[5], (D, QH * HD), D ** -0.5, 0.0625, ((0, 8), (1, 4))),
        "w_keyval": gaussian(splits[6], (D, KVD), (D // 4) ** -0.5, 0.125, ((0, 8), (1, 4))),
    }


def rotate(values, positions):
    midpoint = values.shape[-1] // 2
    frequency = jnp.exp(jnp.arange(midpoint, dtype=jnp.float32) * (-2.0 * math.log(500000.0) / values.shape[-1]))
    angles = positions.astype(jnp.float32)[:, None] * frequency[None, :]
    cosine = jnp.cos(angles)[:, None, :]
    sine_term = jnp.sin(angles)[:, None, :]
    leading = values[..., :midpoint]
    trailing = values[..., midpoint:]
    return jnp.concatenate((leading * cosine - trailing * sine_term, trailing * cosine + leading * sine_term), axis=-1)

def normalize(states):
    floated = states.astype(jnp.float32)
    return (floated * lax.rsqrt(lax.optimization_barrier(jnp.mean(floated * floated, axis=-1, keepdims=True)) + 1e-05)).astype(jnp.bfloat16)

def reference(store_kv, block_slot, block_owner, rec_pos, states, w_query, w_keyval):

    def request(inputs):
        slot_ids, owners, positions, hidden = inputs
        blocks = store_kv[owners * SB + slot_ids].reshape(CTX, KVD)
        normed = normalize(hidden)
        query_raw = jnp.dot(normed, w_query, preferred_element_type=jnp.float32).reshape(REC, QH, HD)
        queries = (rotate(query_raw, positions) * HD ** (-0.5)).astype(jnp.bfloat16)
        fresh = jnp.dot(normed, w_keyval, preferred_element_type=jnp.float32).astype(jnp.bfloat16)
        fresh_key = rotate(fresh[:, :KVH * HD].astype(jnp.float32).reshape(REC, KVH, HD), positions).astype(jnp.bfloat16)
        replaced = jnp.concatenate((fresh_key.reshape(REC, KVH * HD), fresh[:, KVH * HD:]), axis=1)
        assembled = blocks.at[positions].set(replaced)
        key_rows = assembled[:, :KVH * HD].reshape(CTX, KVH, HD).astype(jnp.float32)
        value_rows = assembled[:, KVH * HD:].reshape(CTX, KVH, HD).astype(jnp.float32)
        grouped = queries.reshape(REC, KVH, QH // KVH, HD).astype(jnp.float32)
        scores = jnp.einsum('rkgd,ckd->kgrc', grouped, key_rows)
        visible = jnp.arange(CTX)[None, :] <= positions[:, None]
        scores = jnp.where(visible[None, None], scores, -1e+30)
        row_max = lax.optimization_barrier(jnp.max(scores, axis=-1, keepdims=True))
        exponent = jnp.exp(scores - row_max)
        weights = (exponent / lax.optimization_barrier(jnp.sum(exponent, axis=-1, keepdims=True))).astype(jnp.bfloat16)
        attended = jnp.einsum('kgrc,ckd->rkgd', weights.astype(jnp.float32), value_rows)
        return attended.reshape(REC, QH * HD).astype(jnp.bfloat16)
    return lax.map(request, (block_slot, block_owner, rec_pos, states))
```

```python
import functools
import math

import jax
import jax.numpy as jnp
from jax import lax
from jax.experimental import pallas as pl
from jax.experimental.pallas import tpu as pltpu
from jax.sharding import PartitionSpec as P

QH = 32
KVH = 4
HD = 128
CAP = 2
F32 = jnp.float32
BF16 = jnp.bfloat16


def rotate(values, positions):
    midpoint = values.shape[-1] // 2
    frequency = jnp.exp(
        jnp.arange(midpoint, dtype=jnp.float32) * (-2.0 * math.log(500000.0) / values.shape[-1])
    )
    angles = positions.astype(jnp.float32)[:, None] * frequency[None, :]
    cosine = jnp.cos(angles)[:, None, :]
    sine_term = jnp.sin(angles)[:, None, :]
    leading = values[..., :midpoint]
    trailing = values[..., midpoint:]
    return jnp.concatenate(
        (leading * cosine - trailing * sine_term, trailing * cosine + leading * sine_term), axis=-1
    )


def normalize(states):
    floated = states.astype(jnp.float32)
    return (
        floated * lax.rsqrt(jnp.mean(floated * floated, axis=-1, keepdims=True) + 1e-05)
    ).astype(jnp.bfloat16)


def fetch_blocks(store_kv, slot_ids, owners):
    store_count = lax.axis_size("store")
    piece_rows = store_kv.shape[1]
    row_width = store_kv.shape[2]
    block_count = slot_ids.shape[0]
    slot_order = jnp.arange(block_count)
    earlier = slot_order[None, :] < slot_order[:, None]
    slot_ranks = jnp.sum((owners[:, None] == owners[None, :]) & earlier, axis=1)
    slot_hits = (owners[:, None, None] == jnp.arange(store_count)[None, :, None]) & (
        slot_ranks[:, None, None] == jnp.arange(CAP)[None, None, :]
    )
    wanted = jnp.sum(jnp.where(slot_hits, slot_ids[:, None, None], 0), axis=0)
    arrived = lax.all_to_all(
        store_kv[lax.all_to_all(wanted, "store", split_axis=0, concat_axis=0, tiled=True)],
        "store",
        split_axis=0,
        concat_axis=0,
        tiled=True,
    )
    return arrived.reshape(store_count * CAP, piece_rows, row_width)[
        owners * CAP + slot_ranks
    ].reshape(block_count * piece_rows, row_width)


def general_body(store_kv, block_slot, block_owner, rec_pos, states, w_query, w_keyval):
    ctx_count = lax.axis_size("ctx")
    my_index = lax.axis_index("ctx")
    piece_rows = store_kv.shape[1]
    block_count = block_slot.shape[1]
    rec_count = rec_pos.shape[1]
    positions = rec_pos[0]
    shard_rows = block_count * piece_rows
    local_rows = fetch_blocks(store_kv, block_slot[0], block_owner[0])
    normed = normalize(states[0])
    query_cols = w_query.shape[1]
    query_weight, keyval_weight = (
        lax.all_gather(w_query, "store", axis=0, tiled=True),
        lax.all_gather(w_keyval, "store", axis=0, tiled=True),
    )
    row_piece = lax.all_gather(normed, "ctx", axis=0, tiled=True)
    query_raw = jnp.dot(row_piece, query_weight, preferred_element_type=jnp.float32)
    keyval_raw = jnp.dot(row_piece, keyval_weight, preferred_element_type=jnp.float32)
    heads_here = query_cols // HD
    group_size = QH // KVH
    queries = (
        rotate(query_raw.reshape(rec_count, heads_here, HD), positions) * HD ** (-0.5)
    ).astype(jnp.bfloat16)
    fresh_rows = lax.all_gather(keyval_raw.astype(jnp.bfloat16), "ctx", axis=1, tiled=True)
    shared_head = my_index * heads_here // group_size
    fresh_key = rotate(
        lax.dynamic_slice_in_dim(fresh_rows, shared_head * HD, HD, 1)
        .astype(jnp.float32)
        .reshape(rec_count, 1, HD),
        positions,
    )
    fresh_key = fresh_key.astype(jnp.bfloat16).reshape(rec_count, HD)
    fresh_value = lax.dynamic_slice_in_dim(fresh_rows, KVH * HD + shared_head * HD, HD, 1)
    gathered = lax.all_gather(local_rows, "ctx", axis=0, tiled=True)
    key_rows = lax.dynamic_slice_in_dim(gathered, shared_head * HD, HD, 1)
    value_rows = lax.dynamic_slice_in_dim(gathered, KVH * HD + shared_head * HD, HD, 1)
    row_ids = jnp.arange(ctx_count * shard_rows)
    block_len = piece_rows * ctx_count
    key_pos = (
        row_ids % shard_rows // piece_rows * block_len
        + row_ids // shard_rows * piece_rows
        + row_ids % piece_rows
    )
    targets = (
        positions % block_len // piece_rows * shard_rows
        + positions // block_len * piece_rows
        + positions % piece_rows
    )
    key_rows = key_rows.at[targets].set(fresh_key)
    value_rows = value_rows.at[targets].set(fresh_value)
    scores = jnp.einsum("rhd,cd->hrc", queries, key_rows, preferred_element_type=jnp.float32)
    visible = key_pos[None, None, :] <= positions[None, :, None]
    scores = jnp.where(visible, scores, -1e30)
    row_max = jnp.max(scores, axis=-1, keepdims=True)
    exponent = jnp.exp(scores - row_max)
    weights = (exponent / jnp.sum(exponent, axis=-1, keepdims=True)).astype(jnp.bfloat16)
    attended = jnp.einsum("hrc,cd->rhd", weights, value_rows, preferred_element_type=jnp.float32)
    return attended.reshape(1, rec_count, heads_here * HD).astype(jnp.bfloat16)


CORE, XBIT, YBIT = 1, 2, 4


def flip(bit, count):
    return [(s, s ^ bit) for s in range(count)]


def norm_kernel(states_ref, keep_ref, send_ref):
    me = lax.axis_index("store")
    width = states_ref.shape[1]
    depth = width // 8
    total = jnp.zeros((states_ref.shape[0], 1), F32)
    for s in range(8):
        part = states_ref[:, s * depth : (s + 1) * depth].astype(F32)
        total += jnp.sum(part * part, axis=1, keepdims=True)
    scale = lax.rsqrt(total / width + 1e-05)
    for r in range(4):
        for core, out in ((0, keep_ref), (1, send_ref)):
            s = lax.bitwise_xor(me, r * 2 + core)
            part = states_ref[:, pl.ds(pl.multiple_of(s * depth, depth), depth)].astype(F32)
            out[:, r * depth : (r + 1) * depth] = (part * scale).astype(BF16)


def norm_split(states):
    rows, width = states.shape
    half = jax.ShapeDtypeStruct((rows, width // 2), BF16)
    return pl.pallas_call(
        norm_kernel,
        out_shape=(half, half),
        compiler_params=pltpu.CompilerParams(vmem_limit_bytes=16 << 20),
        name="norm_split",
    )(states)


def project_kernel(count, rows, depth, *refs):
    n_a = 2 * (2 * count - 1)
    a_refs = refs[:n_a]
    w_own, w_x, w_y, w_dx, w_dy = refs[n_a : n_a + 5]
    out_own, out_sib, a_buf, sems = refs[n_a + 5 :]
    me = lax.axis_index("ctx")

    def copies(act):
        index = 0
        for side in range(2):
            for step in range(count):
                for sign in (-1, 1):
                    if step == 0 and sign == 1:
                        continue
                    source = a_refs[index]
                    sem = sems.at[index]
                    index += 1
                    shard = me + sign * step
                    ok = (shard >= 0) & (shard < count)

                    @pl.when(ok)
                    def _():
                        start = pl.multiple_of(side * count * rows + shard * rows, rows)
                        act(pltpu.make_async_copy(source, a_buf.at[pl.ds(start, rows)], sem))

    copies(lambda c: c.start())
    copies(lambda c: c.wait())
    total = jnp.dot(a_buf[:, :depth], w_own[...], preferred_element_type=F32)
    total += jnp.dot(a_buf[:, depth : 2 * depth], w_x[...], preferred_element_type=F32)
    total += jnp.dot(a_buf[:, 2 * depth : 3 * depth], w_y[...], preferred_element_type=F32)
    h = depth // 2
    total += jnp.dot(a_buf[:, 3 * depth : 3 * depth + h], w_dx[...], preferred_element_type=F32)
    total += jnp.dot(a_buf[:, 3 * depth + h :], w_dy[...], preferred_element_type=F32)
    half = total.shape[0] // 2
    out_own[...] = total[:half]
    out_sib[...] = total[half:]


def project(a_parts, w_own, w_x, w_y, w_dx, w_dy, chunk, cols):
    count = (len(a_parts) // 2 + 1) // 2
    rows, width = a_parts[0].shape
    depth = w_own.shape[0]
    anyspec = pl.BlockSpec(memory_space=pl.ANY)
    wspec = pl.BlockSpec((depth, cols), lambda i: (0, chunk))
    dspec = pl.BlockSpec((depth // 2, cols), lambda i: (0, 0))
    out = jax.ShapeDtypeStruct((count * rows, cols), F32)
    ospec = pl.BlockSpec((count * rows, cols), lambda i: (0, 0))
    return pl.pallas_call(
        functools.partial(project_kernel, count, rows, depth),
        grid=(1,),
        in_specs=[anyspec] * len(a_parts) + [wspec] * 3 + [dspec] * 2,
        out_specs=(ospec, ospec),
        out_shape=(out, out),
        scratch_shapes=[
            pltpu.VMEM((2 * count * rows, width), BF16),
            pltpu.SemaphoreType.DMA((len(a_parts),)),
        ],
        compiler_params=pltpu.CompilerParams(vmem_limit_bytes=40 << 20),
        cost_estimate=pl.CostEstimate(
            flops=4 * count * rows * width * cols,
            bytes_accessed=4 * count * rows * width + 2 * width * cols,
            transcendentals=0,
        ),
        name="project",
    )(*a_parts, w_own, w_x, w_y, w_dx, w_dy)


def turn(values, cosine, sine):
    return values * cosine + pltpu.roll(values, HD // 2, 1) * sine


def assemble_kernel(own_ref, sib_ref, cached_ref, cos_ref, sin_ref, target_ref, key_ref, value_ref):
    fresh = (own_ref[...] + sib_ref[...]).astype(BF16)
    fresh_key = turn(fresh[:, :HD].astype(F32), cos_ref[...], sin_ref[...]).astype(BF16)
    context = cached_ref.shape[0]
    count = fresh.shape[0]
    hit = lax.broadcasted_iota(jnp.int32, (context, count), 0) == target_ref[...]
    pick = jnp.where(hit, 1.0, 0.0)
    taken = jnp.max(pick, axis=1, keepdims=True) > 0.5
    pick = pick.astype(BF16)
    key_new = jnp.dot(pick, fresh_key, preferred_element_type=F32).astype(BF16)
    value_new = jnp.dot(pick, fresh[:, HD:], preferred_element_type=F32).astype(BF16)
    key_ref[...] = jnp.where(taken, key_new, cached_ref[:, :HD])
    value_ref[...] = jnp.where(taken, value_new, cached_ref[:, HD:])


def assemble(own, sib, cached, cosine, sine, targets):
    out = jax.ShapeDtypeStruct((cached.shape[0], HD), BF16)
    return pl.pallas_call(
        assemble_kernel,
        out_shape=(out, out),
        compiler_params=pltpu.CompilerParams(vmem_limit_bytes=16 << 20),
        name="assemble",
    )(own, sib, cached, cosine, sine, targets)


def attend_kernel(shard_rows, piece_rows, block_len, heads, *refs):
    own_ref, sib_ref, key_ref, value_ref, cos_ref, sin_ref, pos_ref, *rest = refs
    out_ref = rest[-1]
    row = lax.broadcasted_iota(jnp.int32, (1, key_ref.shape[0]), 1)
    key_pos = (
        row % shard_rows // piece_rows * block_len
        + row // shard_rows * piece_rows
        + row % piece_rows
    )
    visible = key_pos <= pos_ref[...]
    for h in range(heads):
        cols = slice(h * HD, (h + 1) * HD)
        raw = own_ref[:, cols] + sib_ref[:, cols]
        query = (turn(raw, cos_ref[...], sin_ref[...]) * HD ** (-0.5)).astype(BF16)
        scores = lax.dot_general(
            query, key_ref[...], (((1,), (1,)), ((), ())), preferred_element_type=F32
        )
        scores = jnp.where(visible, scores, -1e30)
        exponent = jnp.exp(scores - jnp.max(scores, axis=1, keepdims=True))
        weights = (exponent / jnp.sum(exponent, axis=1, keepdims=True)).astype(BF16)
        out_ref[:, cols] = jnp.dot(weights, value_ref[...], preferred_element_type=F32).astype(BF16)


def attend(own, sib, key_rows, value_rows, cosine, sine, pos_col, layout, chunk, width, before):
    rec_count, cols = own.shape
    whole = lambda a: pl.BlockSpec(a.shape, lambda i: (0, 0))
    args = [own, sib, key_rows, value_rows, cosine, sine, pos_col]
    specs = [whole(a) for a in args]
    aliases = {}
    if before is not None:
        aliases = {len(args): 0}
        args.append(before)
        specs.append(pl.BlockSpec(memory_space=pl.ANY))
    return pl.pallas_call(
        functools.partial(attend_kernel, *layout, cols // HD),
        grid=(1,),
        in_specs=specs,
        out_specs=pl.BlockSpec((rec_count, cols), lambda i: (0, chunk)),
        out_shape=jax.ShapeDtypeStruct((rec_count, width), BF16),
        input_output_aliases=aliases,
        compiler_params=pltpu.CompilerParams(vmem_limit_bytes=32 << 20),
        name="attend",
    )(*args)


def fast_body(store_kv, block_slot, block_owner, rec_pos, states, w_query, w_keyval):
    store_count = lax.axis_size("store")
    ctx_count = lax.axis_size("ctx")
    my_index = lax.axis_index("ctx")
    piece_rows = store_kv.shape[1]
    block_count = block_slot.shape[1]
    rec_count = rec_pos.shape[1]
    query_cols = w_query.shape[1]
    depth = w_query.shape[0]
    positions = rec_pos[0]
    xf, yf, cf = (flip(b, store_count) for b in (XBIT, YBIT, CORE))
    by_x = lambda a: lax.ppermute(a, "store", xf)
    by_y = lambda a: lax.ppermute(a, "store", yf)
    by_core = lambda a: lax.ppermute(a, "store", cf)

    wq_x = by_x(w_query)
    wq_y = by_y(w_query)

    low, high = w_keyval[:, :HD], w_keyval[:, HD:]
    first = lax.ppermute(jnp.where(my_index == 0, high, low), "ctx", [(0, 1), (1, 2), (2, 0)])
    second = lax.ppermute(jnp.where(my_index == 3, low, high), "ctx", [(1, 3), (2, 1), (3, 2)])
    key_w = jnp.where(my_index == 0, low, jnp.where(my_index == 3, second, first))
    value_w = jnp.where(my_index == 0, first, jnp.where(my_index == 3, high, second))
    wkv = jnp.concatenate((key_w, value_w), axis=1)

    keep, send = norm_split(states[0])
    other = by_core(send)
    a_parts = []
    for shard in (keep, other):
        ups, downs = [shard], [shard]
        for step in range(1, ctx_count):
            ups.append(
                lax.ppermute(ups[-1], "ctx", [(i, i + 1) for i in range(step - 1, ctx_count - 1)])
            )
            downs.append(
                lax.ppermute(downs[-1], "ctx", [(i, i - 1) for i in range(1, ctx_count - step + 1)])
            )
        a_parts.append(ups[0])
        for step in range(1, ctx_count):
            a_parts += [ups[step], downs[step]]

    wkv_x = by_x(wkv)
    wkv_y = by_y(wkv)

    local_rows = fetch_blocks(store_kv, block_slot[0], block_owner[0])
    shard_rows = block_count * piece_rows
    by_head = jnp.stack(
        [
            jnp.concatenate(
                (
                    local_rows[:, h * HD : (h + 1) * HD],
                    local_rows[:, (KVH + h) * HD : (KVH + h + 1) * HD],
                ),
                axis=1,
            )
            for h in range(ctx_count)
        ]
    )
    cached = lax.all_to_all(by_head, "ctx", split_axis=0, concat_axis=0, tiled=True)
    cached = cached.reshape(ctx_count * shard_rows, 2 * HD)

    frequency = jnp.exp(
        jnp.arange(HD // 2, dtype=F32) * (-2.0 * math.log(500000.0) / HD)
    )
    angles = positions.astype(F32)[:, None] * frequency[None, :]
    cos_half, sin_half = jnp.cos(angles), jnp.sin(angles)
    cosine = jnp.concatenate((cos_half, cos_half), axis=1)
    sine = jnp.concatenate((-sin_half, sin_half), axis=1)
    block_len = piece_rows * ctx_count
    targets = (
        positions % block_len // piece_rows * shard_rows
        + positions // block_len * piece_rows
        + positions % piece_rows
    )

    half = depth // 2
    chunk_cols = 2 * HD

    def diagonal(from_x, from_y, chunk):
        cols = slice(chunk * chunk_cols, (chunk + 1) * chunk_cols)
        return by_x(from_y[:half, cols]), by_y(from_x[half:, cols])

    own, sib = project(a_parts, wkv, wkv_x, wkv_y, *diagonal(wkv_x, wkv_y, 0), 0, chunk_cols)
    key_rows, value_rows = assemble(
        own, by_core(sib), cached, cosine, sine, targets.reshape(1, rec_count)
    )
    result = None
    for chunk in range(query_cols // chunk_cols):
        own, sib = project(
            a_parts, w_query, wq_x, wq_y, *diagonal(wq_x, wq_y, chunk), chunk, chunk_cols
        )
        result = attend(
            own,
            by_core(sib),
            key_rows,
            value_rows,
            cosine,
            sine,
            positions.reshape(rec_count, 1),
            (shard_rows, piece_rows, block_len),
            chunk,
            query_cols,
            result,
        )
    return result.reshape(1, rec_count, query_cols)


def solution(mesh):
    fast = mesh.shape["store"] == 8 and mesh.shape["ctx"] == KVH
    return jax.shard_map(
        fast_body if fast else general_body,
        mesh=mesh,
        in_specs=(
            P("store", "ctx", None),
            P("store", None),
            P("store", None),
            P("store", None),
            P("store", "ctx", None),
            P("store", "ctx"),
            P("store", "ctx"),
        ),
        out_specs=P("store", None, "ctx"),
        check_vma=False,
    )
```

```python
import functools
import math

import jax
import jax.numpy as jnp
from jax import lax
from jax.experimental import pallas as pl
from jax.experimental.pallas import tpu as pltpu
from jax.sharding import PartitionSpec as P

QH = 32
KVH = 4
HD = 128
CAP = 2
F32 = jnp.float32
BF16 = jnp.bfloat16


def rotate(values, positions):
    midpoint = values.shape[-1] // 2
    frequency = jnp.exp(
        jnp.arange(midpoint, dtype=jnp.float32) * (-2.0 * math.log(500000.0) / values.shape[-1])
    )
    angles = positions.astype(jnp.float32)[:, None] * frequency[None, :]
    cosine = jnp.cos(angles)[:, None, :]
    sine_term = jnp.sin(angles)[:, None, :]
    leading = values[..., :midpoint]
    trailing = values[..., midpoint:]
    return jnp.concatenate(
        (leading * cosine - trailing * sine_term, trailing * cosine + leading * sine_term), axis=-1
    )


def normalize(states):
    floated = states.astype(jnp.float32)
    return (
        floated * lax.rsqrt(jnp.mean(floated * floated, axis=-1, keepdims=True) + 1e-05)
    ).astype(jnp.bfloat16)


def swap_ids(slot_ids, owners, store_count):
    block_count = slot_ids.shape[0]
    slot_order = jnp.arange(block_count)
    earlier = slot_order[None, :] < slot_order[:, None]
    slot_ranks = jnp.sum((owners[:, None] == owners[None, :]) & earlier, axis=1)
    slot_hits = (owners[:, None, None] == jnp.arange(store_count)[None, :, None]) & (
        slot_ranks[:, None, None] == jnp.arange(CAP)[None, None, :]
    )
    wanted = jnp.sum(jnp.where(slot_hits, slot_ids[:, None, None], 0), axis=0)
    asked = lax.all_to_all(wanted, "store", split_axis=0, concat_axis=0, tiled=True)
    return asked, owners * CAP + slot_ranks


def fetch_blocks(store_kv, asked, places):
    arrived = lax.all_to_all(store_kv[asked], "store", split_axis=0, concat_axis=0, tiled=True)
    return arrived.reshape((-1,) + store_kv.shape[1:])[places].reshape(-1, store_kv.shape[2])


def general_body(store_kv, block_slot, block_owner, rec_pos, states, w_query, w_keyval):
    ctx_count = lax.axis_size("ctx")
    my_index = lax.axis_index("ctx")
    piece_rows = store_kv.shape[1]
    block_count = block_slot.shape[1]
    rec_count = rec_pos.shape[1]
    positions = rec_pos[0]
    shard_rows = block_count * piece_rows
    local_rows = fetch_blocks(
        store_kv, *swap_ids(block_slot[0], block_owner[0], lax.axis_size("store"))
    )
    normed = normalize(states[0])
    query_cols = w_query.shape[1]
    query_weight, keyval_weight = (
        lax.all_gather(w_query, "store", axis=0, tiled=True),
        lax.all_gather(w_keyval, "store", axis=0, tiled=True),
    )
    row_piece = lax.all_gather(normed, "ctx", axis=0, tiled=True)
    query_raw = jnp.dot(row_piece, query_weight, preferred_element_type=jnp.float32)
    keyval_raw = jnp.dot(row_piece, keyval_weight, preferred_element_type=jnp.float32)
    heads_here = query_cols // HD
    group_size = QH // KVH
    queries = (
        rotate(query_raw.reshape(rec_count, heads_here, HD), positions) * HD ** (-0.5)
    ).astype(jnp.bfloat16)
    fresh_rows = lax.all_gather(keyval_raw.astype(jnp.bfloat16), "ctx", axis=1, tiled=True)
    shared_head = my_index * heads_here // group_size
    fresh_key = rotate(
        lax.dynamic_slice_in_dim(fresh_rows, shared_head * HD, HD, 1)
        .astype(jnp.float32)
        .reshape(rec_count, 1, HD),
        positions,
    )
    fresh_key = fresh_key.astype(jnp.bfloat16).reshape(rec_count, HD)
    fresh_value = lax.dynamic_slice_in_dim(fresh_rows, KVH * HD + shared_head * HD, HD, 1)
    gathered = lax.all_gather(local_rows, "ctx", axis=0, tiled=True)
    key_rows = lax.dynamic_slice_in_dim(gathered, shared_head * HD, HD, 1)
    value_rows = lax.dynamic_slice_in_dim(gathered, KVH * HD + shared_head * HD, HD, 1)
    row_ids = jnp.arange(ctx_count * shard_rows)
    block_len = piece_rows * ctx_count
    key_pos = (
        row_ids % shard_rows // piece_rows * block_len
        + row_ids // shard_rows * piece_rows
        + row_ids % piece_rows
    )
    targets = (
        positions % block_len // piece_rows * shard_rows
        + positions // block_len * piece_rows
        + positions % piece_rows
    )
    key_rows = key_rows.at[targets].set(fresh_key)
    value_rows = value_rows.at[targets].set(fresh_value)
    scores = jnp.einsum("rhd,cd->hrc", queries, key_rows, preferred_element_type=jnp.float32)
    visible = key_pos[None, None, :] <= positions[None, :, None]
    scores = jnp.where(visible, scores, -1e30)
    row_max = jnp.max(scores, axis=-1, keepdims=True)
    exponent = jnp.exp(scores - row_max)
    weights = (exponent / jnp.sum(exponent, axis=-1, keepdims=True)).astype(jnp.bfloat16)
    attended = jnp.einsum("hrc,cd->rhd", weights, value_rows, preferred_element_type=jnp.float32)
    return attended.reshape(1, rec_count, heads_here * HD).astype(jnp.bfloat16)


CORE, XBIT, YBIT = 1, 2, 4


def flip(bit, count):
    return [(s, s ^ bit) for s in range(count)]


def norm_kernel(states_ref, keep_ref, send_ref):
    me = lax.axis_index("store")
    width = states_ref.shape[1]
    depth = width // 8
    total = jnp.zeros((states_ref.shape[0], 1), F32)
    for s in range(8):
        part = states_ref[:, s * depth : (s + 1) * depth].astype(F32)
        total += jnp.sum(part * part, axis=1, keepdims=True)
    scale = lax.rsqrt(total / width + 1e-05)
    for r in range(4):
        for core, out in ((0, keep_ref), (1, send_ref)):
            s = lax.bitwise_xor(me, r * 2 + core)
            part = states_ref[:, pl.ds(pl.multiple_of(s * depth, depth), depth)].astype(F32)
            out[:, r * depth : (r + 1) * depth] = (part * scale).astype(BF16)


def norm_split(states):
    rows, width = states.shape
    half = jax.ShapeDtypeStruct((rows, width // 2), BF16)
    return pl.pallas_call(
        norm_kernel,
        out_shape=(half, half),
        compiler_params=pltpu.CompilerParams(vmem_limit_bytes=16 << 20),
        name="norm_split",
    )(states)


def cut_kernel(plan, n_in, *refs):
    outs, sems = refs[n_in:-1], refs[-1]
    copies = []
    for out, pieces in zip(outs, plan):
        for source, (row, col), (to_row, to_col), (rows, cols) in pieces:
            copies.append(
                pltpu.make_async_copy(
                    refs[source].at[pl.ds(row, rows), pl.ds(col, cols)],
                    out.at[pl.ds(to_row, rows), pl.ds(to_col, cols)],
                    sems.at[len(copies)],
                )
            )
    for copy in copies:
        copy.start()
    for copy in copies:
        copy.wait()


def cut(sources, plan, shapes, gates=(), near=False):
    args = [*sources, *jax.tree.leaves(gates)]
    hbm = pl.BlockSpec(memory_space=pltpu.HBM)
    vmem = pl.BlockSpec(memory_space=pltpu.VMEM)
    return pl.pallas_call(
        functools.partial(cut_kernel, plan, len(args)),
        in_specs=[vmem if near else hbm] * len(args),
        out_specs=[hbm if near else vmem] * len(shapes),
        out_shape=[jax.ShapeDtypeStruct(shape, BF16) for shape in shapes],
        scratch_shapes=[pltpu.SemaphoreType.DMA((sum(len(p) for p in plan),))],
        compiler_params=pltpu.CompilerParams(vmem_limit_bytes=8 << 20),
        name="cut",
    )(*args)


def relay_kernel(own, two, up, down, sems):
    me = lax.axis_index("ctx")

    def moves(act):
        for way, out in enumerate((up, down)):
            for source, chosen in ((own, me == 1 + way), (two, me != 1 + way)):

                @pl.when(chosen)
                def _():
                    act(pltpu.make_async_copy(source, out, sems.at[way]))

    moves(lambda c: c.start())
    moves(lambda c: c.wait())


def relay(own, two):
    hbm = pl.BlockSpec(memory_space=pltpu.HBM)
    out = jax.ShapeDtypeStruct(own.shape, BF16)
    return pl.pallas_call(
        relay_kernel,
        in_specs=[hbm] * 2,
        out_shape=(out, out),
        scratch_shapes=[pltpu.SemaphoreType.DMA((2,))],
        compiler_params=pltpu.CompilerParams(vmem_limit_bytes=4 << 20),
        name="relay",
    )(own, two)


def sort_kernel(blocks_ref, places_ref, *refs):
    out_ref = refs[-1]
    heads = out_ref.shape[0]
    size = blocks_ref.shape[1]
    for j in range(places_ref.shape[0]):
        block = blocks_ref[places_ref[j]]
        for h in range(heads):
            rows = slice(j * size, (j + 1) * size)
            out_ref[h, rows, :HD] = block[:, h * HD : (h + 1) * HD]
            out_ref[h, rows, HD:] = block[:, (heads + h) * HD : (heads + h + 1) * HD]


def sort_blocks(blocks, places, gates):
    hbm = pl.BlockSpec(memory_space=pltpu.HBM)
    count, size, _ = blocks.shape
    return pl.pallas_call(
        sort_kernel,
        in_specs=[pl.BlockSpec(memory_space=pltpu.VMEM), pl.BlockSpec(memory_space=pltpu.SMEM)]
        + [hbm] * len(gates),
        out_shape=jax.ShapeDtypeStruct((KVH, places.shape[0] * size, 2 * HD), BF16),
        compiler_params=pltpu.CompilerParams(vmem_limit_bytes=4 << 20),
        name="sort_blocks",
    )(blocks, places, *gates)


STEP = 2 * HD


def share(total, shards, own, sib, cols):
    rows = own.shape[0] // shards
    for z in range(shards):
        here = slice(z * rows, (z + 1) * rows)
        own[here, cols] = total[2 * z * rows : (2 * z + 1) * rows]
        sib[here, cols] = total[(2 * z + 1) * rows : (2 * z + 2) * rows]


def project_kernel(shards, slices, chunks, n_weights, started, n_gates, *refs):
    a_refs, w_refs = refs[:5], refs[5 : 5 + n_weights]
    refs = refs[5 + n_weights :]
    before = refs[0] if started else None
    outs = refs[started + n_gates : -5]
    a_buf, w_buf, acc, a_sems, w_sems = refs[-5:]
    me = lax.axis_index("ctx")
    depth = a_buf.shape[2]
    rows = a_buf.shape[1] // shards

    def row_copies(index, act):
        cols = pl.ds(slices[index] * depth, depth)
        for k in range(4):
            start = pl.multiple_of(lax.bitwise_xor(me, k) * rows, rows)
            target = a_buf.at[index, pl.ds(start, rows)]
            sem = a_sems.at[index * 4 + k]
            if k < 3:
                act(pltpu.make_async_copy(a_refs[k].at[:, cols], target, sem))
            else:
                for source, chosen in ((a_refs[3], me >= 2), (a_refs[4], me < 2)):

                    @pl.when(chosen)
                    def _():
                        act(pltpu.make_async_copy(source.at[:, cols], target, sem))

    weight_copies = {}
    count = 0
    for index in range(len(slices)):
        row_copies(index, lambda c: c.start())
        for c, (_, pieces) in enumerate(chunks):
            if index >= len(pieces):
                continue
            here, row_to = [], 0
            for ref, row, col, size in pieces[index]:
                here.append(
                    pltpu.make_async_copy(
                        w_refs[ref].at[pl.ds(row, size), pl.ds(col, STEP)],
                        w_buf.at[c, index, pl.ds(row_to, size)],
                        w_sems.at[count],
                    )
                )
                here[-1].start()
                row_to += size
                count += 1
            weight_copies[c, index] = here
    for index in range(len(slices)):
        row_copies(index, lambda c: c.wait())
        for c, (place, pieces) in enumerate(chunks):
            if index >= len(pieces):
                continue
            for copy in weight_copies[c, index]:
                copy.wait()
            part = jnp.dot(a_buf[index], w_buf[c, index], preferred_element_type=F32)
            if index > 0:
                part += acc[c]
            elif started:
                part += before[:, c * STEP : (c + 1) * STEP]
            if index < len(pieces) - 1:
                acc[c] = part
            elif place[1] is None:
                outs[place[0]][:, place[2]] = part
            else:
                share(part, shards, outs[place[0]], outs[place[1]], place[2])


def project(shard_rows, weights, slices, chunks, outs, before=None, gates=()):
    rows, width = shard_rows[0].shape
    depth = width // 4
    shards = 4
    hbm = pl.BlockSpec(memory_space=pltpu.HBM)
    vmem = pl.BlockSpec(memory_space=pltpu.VMEM)
    started = before is not None
    args = [*shard_rows, *weights, *([before] if started else []), *gates]
    n_weight_copies = sum(len(p) for _, pieces in chunks for p in pieces)
    work = sum(len(pieces) for _, pieces in chunks)
    return pl.pallas_call(
        functools.partial(
            project_kernel, shards, slices, chunks, len(weights), started, len(gates)
        ),
        in_specs=[hbm] * (5 + len(weights)) + [vmem] * started + [hbm] * len(gates),
        out_shape=[jax.ShapeDtypeStruct(shape, F32) for shape in outs],
        scratch_shapes=[
            pltpu.VMEM((len(slices), shards * rows, depth), BF16),
            pltpu.VMEM((len(chunks), len(slices), depth, STEP), BF16),
            pltpu.VMEM((len(chunks), shards * rows, STEP), F32),
            pltpu.SemaphoreType.DMA((4 * len(slices),)),
            pltpu.SemaphoreType.DMA((n_weight_copies,)),
        ],
        compiler_params=pltpu.CompilerParams(vmem_limit_bytes=58 << 20),
        cost_estimate=pl.CostEstimate(
            flops=2 * shards * rows * depth * STEP * work,
            bytes_accessed=8 * rows * width,
            transcendentals=0,
        ),
        name="project",
    )(*args)


def turn(values, cosine, sine):
    return values * cosine + pltpu.roll(values, HD // 2, 1) * sine


def assemble_kernel(fresh_ref, first_ref, second_ref, cached_ref, cos_ref, sin_ref, target_ref, key_ref, value_ref):
    me = lax.axis_index("ctx")
    low, high = fresh_ref[:, :HD].astype(F32), fresh_ref[:, HD:].astype(F32)
    first, second = first_ref[...].astype(F32), second_ref[...].astype(F32)
    fresh_key = jnp.where(me == 0, low, jnp.where(me == 3, second, first))
    fresh_value = jnp.where(me == 0, first, jnp.where(me == 3, high, second)).astype(BF16)
    fresh_key = turn(fresh_key, cos_ref[...], sin_ref[...]).astype(BF16)
    context = cached_ref.shape[0]
    count = fresh_key.shape[0]
    hit = lax.broadcasted_iota(jnp.int32, (context, count), 0) == target_ref[...]
    pick = jnp.where(hit, 1.0, 0.0)
    taken = jnp.max(pick, axis=1, keepdims=True) > 0.5
    pick = pick.astype(BF16)
    key_new = jnp.dot(pick, fresh_key, preferred_element_type=F32).astype(BF16)
    value_new = jnp.dot(pick, fresh_value, preferred_element_type=F32).astype(BF16)
    key_ref[...] = jnp.where(taken, key_new, cached_ref[:, :HD])
    value_ref[...] = jnp.where(taken, value_new, cached_ref[:, HD:]).T


def assemble(fresh, first, second, cached, cosine, sine, targets):
    context = cached.shape[0]
    return pl.pallas_call(
        assemble_kernel,
        out_shape=(
            jax.ShapeDtypeStruct((context, HD), BF16),
            jax.ShapeDtypeStruct((HD, context), BF16),
        ),
        compiler_params=pltpu.CompilerParams(vmem_limit_bytes=16 << 20),
        name="assemble",
    )(fresh, first, second, cached, cosine, sine, targets)


def attend_kernel(heads, *refs):
    own_ref, sib_ref, key_ref, value_ref, cos_ref, sin_ref, pos_ref, key_pos_ref, *rest = refs
    out_ref = rest[-1]
    visible = key_pos_ref[...] <= pos_ref[...]
    for h in range(heads):
        cols = slice(h * HD, (h + 1) * HD)
        raw = own_ref[:, cols] + sib_ref[:, cols]
        query = (turn(raw, cos_ref[...], sin_ref[...]) * HD ** (-0.5)).astype(BF16)
        scores = lax.dot_general(
            key_ref[...], query, (((1,), (1,)), ((), ())), preferred_element_type=F32
        )
        scores = jnp.where(visible, scores, -1e30)
        exponent = jnp.exp(scores - jnp.max(scores, axis=0, keepdims=True))
        weights = exponent * (1.0 / jnp.sum(exponent, axis=0, keepdims=True))
        turned = jnp.dot(value_ref[...], weights.astype(BF16), preferred_element_type=F32)
        out_ref[:, cols] = turned.T.astype(BF16)


def attend(own, sib, shared, width, start, before):
    rec_count, cols = own.shape
    args = [own, sib, *shared]
    specs = [pl.BlockSpec(a.shape, lambda i: (0, 0)) for a in args]
    aliases = {}
    if before is not None:
        aliases = {len(args): 0}
        args.append(before)
        specs.append(pl.BlockSpec(memory_space=pltpu.HBM))
    return pl.pallas_call(
        functools.partial(attend_kernel, cols // HD),
        grid=(1,),
        in_specs=specs,
        out_specs=pl.BlockSpec((rec_count, cols), lambda i: (0, start // cols)),
        out_shape=jax.ShapeDtypeStruct((rec_count, width), BF16),
        input_output_aliases=aliases,
        compiler_params=pltpu.CompilerParams(vmem_limit_bytes=16 << 20),
        name="attend",
    )(*args)


def fast_body(store_kv, block_slot, block_owner, rec_pos, states, w_query, w_keyval):
    store_count = lax.axis_size("store")
    ctx_count = lax.axis_size("ctx")
    my_index = lax.axis_index("ctx")
    piece_rows = store_kv.shape[1]
    block_count = block_slot.shape[1]
    rec_count = rec_pos.shape[1]
    query_cols = w_query.shape[1]
    depth = w_query.shape[0]
    positions = rec_pos[0]
    xf, yf, cf = (flip(b, store_count) for b in (XBIT, YBIT, CORE))
    by_x = lambda a: lax.ppermute(a, "store", xf)
    by_y = lambda a: lax.ppermute(a, "store", yf)
    by_core = lambda a: lax.ppermute(a, "store", cf)

    along = lambda a, pairs: lax.ppermute(a, "ctx", pairs)
    kv_cols = w_keyval.shape[1]
    late = query_cols // 2
    early = query_cols - late
    first_cols = kv_cols + early
    half = depth // 2

    (w_first,) = cut(
        (w_keyval, w_query),
        [[(0, (0, 0), (0, 0), (depth, kv_cols)), (1, (0, 0), (0, kv_cols), (depth, early))]],
        [(depth, first_cols)],
    )
    first_x, first_y = by_x(w_first), by_y(w_first)
    asked, places = swap_ids(block_slot[0], block_owner[0], store_count)
    (w_last,) = cut(
        (w_query,), [[(0, (0, early), (0, 0), (depth, late))]], [(depth, late)], (asked,)
    )
    last_x, last_y = by_x(w_last), by_y(w_last)

    keep, send = norm_split(states[0])
    shard, width = keep.shape
    (both,) = cut(
        (keep, by_core(send)),
        [[(0, (0, 0), (0, 0), (shard, width)), (1, (0, 0), (shard, 0), (shard, width))]],
        [(2 * shard, width)],
        near=True,
    )
    along = lambda a, pairs: lax.ppermute(a, "ctx", pairs)
    two = along(both, [(0, 2), (1, 3), (2, 0), (3, 1)])
    one = along(both, [(0, 1), (1, 0), (2, 3), (3, 2)])
    up, down = relay(both, two)
    shard_parts = (
        both,
        one,
        two,
        along(up, [(1, 2), (2, 3)]),
        along(down, [(2, 1), (1, 0)]),
    )

    def diagonal(from_x, from_y):
        cols = from_x.shape[1]
        to_x, to_y = cut(
            (from_y, from_x),
            [[(0, (0, 0), (0, 0), (half, cols))], [(1, (half, 0), (0, 0), (half, cols))]],
            [(half, cols)] * 2,
        )
        return (by_x(to_x), by_y(to_y)), to_x

    diag_first, _ = diagonal(first_x, first_y)
    diag_last, sent_last = diagonal(last_x, last_y)

    arrived = lax.all_to_all(store_kv[asked], "store", split_axis=0, concat_axis=0, tiled=True)
    shard_rows = block_count * piece_rows
    arrived = arrived.reshape((-1,) + store_kv.shape[1:])
    by_head = sort_blocks(arrived, places, (up, sent_last))
    cached = lax.all_to_all(by_head, "ctx", split_axis=0, concat_axis=0, tiled=True)
    cached = cached.reshape(ctx_count * shard_rows, 2 * HD)

    frequency = jnp.exp(
        jnp.arange(HD // 2, dtype=F32) * (-2.0 * math.log(500000.0) / HD)
    )
    angles = positions.astype(F32)[:, None] * frequency[None, :]
    cos_half, sin_half = jnp.cos(angles), jnp.sin(angles)
    cosine = jnp.concatenate((cos_half, cos_half), axis=1)
    sine = jnp.concatenate((-sin_half, sin_half), axis=1)
    block_len = piece_rows * ctx_count
    targets = (
        positions % block_len // piece_rows * shard_rows
        + positions // block_len * piece_rows
        + positions % piece_rows
    )

    row_ids = jnp.arange(ctx_count * shard_rows)
    key_pos = (
        row_ids % shard_rows // piece_rows * block_len
        + row_ids // shard_rows * piece_rows
        + row_ids % piece_rows
    )

    def pieces(own, own_col, near, col):
        whole = [[(own, 0, own_col, depth)], [(near, 0, col, depth)], [(near + 1, 0, col, depth)]]
        return whole, whole + [[(near + 2, 0, col, half), (near + 3, 0, col, half)]]

    kv_own, kv_sib = project(
        shard_parts,
        (w_keyval, first_x, first_y, *diag_first),
        (0, 1, 2, 3),
        [((0, 1, slice(0, STEP)), pieces(0, 0, 1, 0)[1])],
        [(rec_count, kv_cols)] * 2,
    )
    chunks = []
    for col in range(0, early, STEP):
        chunks.append(((0, 1, slice(col, col + STEP)), pieces(0, col, 1, kv_cols + col)[1]))
    for col in range(0, late, STEP):
        chunks.append(((2, None, slice(col, col + STEP)), pieces(0, early + col, 5, col)[0]))
    early_own, early_sib, rest = project(
        shard_parts,
        (w_query, first_x, first_y, *diag_first, last_x, last_y),
        (0, 1, 2, 3),
        chunks,
        [(rec_count, early)] * 2 + [(2 * rec_count, late)],
        gates=(kv_sib,),
    )
    fresh = (kv_own + by_core(kv_sib)).astype(BF16)
    low, high = fresh[:, :HD], fresh[:, HD:]
    first = along(jnp.where(my_index == 0, high, low), [(0, 1), (1, 2), (2, 0)])
    second = along(jnp.where(my_index == 3, low, high), [(1, 3), (2, 1), (3, 2)])
    key_rows, value_rows = assemble(
        fresh, first, second, cached, cosine, sine, targets.reshape(1, rec_count)
    )
    shared = (
        key_rows,
        value_rows,
        cosine,
        sine,
        positions.reshape(1, rec_count),
        key_pos.reshape(-1, 1),
    )
    result = attend(early_own, by_core(early_sib), shared, query_cols, 0, None)
    own, sib = project(
        shard_parts,
        diag_last,
        (3,),
        [
            ((0, 1, slice(col, col + STEP)), [[(0, 0, col, half), (1, 0, col, half)]])
            for col in range(0, late, STEP)
        ],
        [(rec_count, late)] * 2,
        before=rest,
    )
    result = attend(own, by_core(sib), shared, query_cols, early, result)
    return result.reshape(1, rec_count, query_cols)


def solution(mesh):
    fast = mesh.shape["store"] == 8 and mesh.shape["ctx"] == KVH
    return jax.shard_map(
        fast_body if fast else general_body,
        mesh=mesh,
        in_specs=(
            P("store", "ctx", None),
            P("store", None),
            P("store", None),
            P("store", None),
            P("store", "ctx", None),
            P("store", "ctx"),
            P("store", "ctx"),
        ),
        out_specs=P("store", None, "ctx"),
        check_vma=False,
    )
```

```python
import functools
import math

import jax
import jax.numpy as jnp
from jax import lax
from jax.experimental import pallas as pl
from jax.experimental.pallas import tpu as pltpu
from jax.sharding import PartitionSpec as P

QH = 32
KVH = 4
HD = 128
CAP = 2
F32 = jnp.float32
BF16 = jnp.bfloat16
TINY = pl.CostEstimate(flops=1, bytes_accessed=1, transcendentals=0)


def rotate(values, positions):
    midpoint = values.shape[-1] // 2
    frequency = jnp.exp(
        jnp.arange(midpoint, dtype=jnp.float32) * (-2.0 * math.log(500000.0) / values.shape[-1])
    )
    angles = positions.astype(jnp.float32)[:, None] * frequency[None, :]
    cosine = jnp.cos(angles)[:, None, :]
    sine_term = jnp.sin(angles)[:, None, :]
    leading = values[..., :midpoint]
    trailing = values[..., midpoint:]
    return jnp.concatenate(
        (leading * cosine - trailing * sine_term, trailing * cosine + leading * sine_term), axis=-1
    )


def normalize(states):
    floated = states.astype(jnp.float32)
    return (
        floated * lax.rsqrt(jnp.mean(floated * floated, axis=-1, keepdims=True) + 1e-05)
    ).astype(jnp.bfloat16)


def swap_ids(slot_ids, owners, store_count):
    block_count = slot_ids.shape[0]
    slot_order = jnp.arange(block_count)
    earlier = slot_order[None, :] < slot_order[:, None]
    slot_ranks = jnp.sum((owners[:, None] == owners[None, :]) & earlier, axis=1)
    slot_hits = (owners[:, None, None] == jnp.arange(store_count)[None, :, None]) & (
        slot_ranks[:, None, None] == jnp.arange(CAP)[None, None, :]
    )
    wanted = jnp.sum(jnp.where(slot_hits, slot_ids[:, None, None], 0), axis=0)
    asked = lax.all_to_all(wanted, "store", split_axis=0, concat_axis=0, tiled=True)
    return asked, owners * CAP + slot_ranks


def fetch_blocks(store_kv, asked, places):
    arrived = lax.all_to_all(store_kv[asked], "store", split_axis=0, concat_axis=0, tiled=True)
    return arrived.reshape((-1,) + store_kv.shape[1:])[places].reshape(-1, store_kv.shape[2])


def general_body(store_kv, block_slot, block_owner, rec_pos, states, w_query, w_keyval):
    ctx_count = lax.axis_size("ctx")
    my_index = lax.axis_index("ctx")
    piece_rows = store_kv.shape[1]
    block_count = block_slot.shape[1]
    rec_count = rec_pos.shape[1]
    positions = rec_pos[0]
    shard_rows = block_count * piece_rows
    local_rows = fetch_blocks(
        store_kv, *swap_ids(block_slot[0], block_owner[0], lax.axis_size("store"))
    )
    normed = normalize(states[0])
    query_cols = w_query.shape[1]
    query_weight, keyval_weight = (
        lax.all_gather(w_query, "store", axis=0, tiled=True),
        lax.all_gather(w_keyval, "store", axis=0, tiled=True),
    )
    row_piece = lax.all_gather(normed, "ctx", axis=0, tiled=True)
    query_raw = jnp.dot(row_piece, query_weight, preferred_element_type=jnp.float32)
    keyval_raw = jnp.dot(row_piece, keyval_weight, preferred_element_type=jnp.float32)
    heads_here = query_cols // HD
    group_size = QH // KVH
    queries = (
        rotate(query_raw.reshape(rec_count, heads_here, HD), positions) * HD ** (-0.5)
    ).astype(jnp.bfloat16)
    fresh_rows = lax.all_gather(keyval_raw.astype(jnp.bfloat16), "ctx", axis=1, tiled=True)
    shared_head = my_index * heads_here // group_size
    fresh_key = rotate(
        lax.dynamic_slice_in_dim(fresh_rows, shared_head * HD, HD, 1)
        .astype(jnp.float32)
        .reshape(rec_count, 1, HD),
        positions,
    )
    fresh_key = fresh_key.astype(jnp.bfloat16).reshape(rec_count, HD)
    fresh_value = lax.dynamic_slice_in_dim(fresh_rows, KVH * HD + shared_head * HD, HD, 1)
    gathered = lax.all_gather(local_rows, "ctx", axis=0, tiled=True)
    key_rows = lax.dynamic_slice_in_dim(gathered, shared_head * HD, HD, 1)
    value_rows = lax.dynamic_slice_in_dim(gathered, KVH * HD + shared_head * HD, HD, 1)
    row_ids = jnp.arange(ctx_count * shard_rows)
    block_len = piece_rows * ctx_count
    key_pos = (
        row_ids % shard_rows // piece_rows * block_len
        + row_ids // shard_rows * piece_rows
        + row_ids % piece_rows
    )
    targets = (
        positions % block_len // piece_rows * shard_rows
        + positions // block_len * piece_rows
        + positions % piece_rows
    )
    key_rows = key_rows.at[targets].set(fresh_key)
    value_rows = value_rows.at[targets].set(fresh_value)
    scores = jnp.einsum("rhd,cd->hrc", queries, key_rows, preferred_element_type=jnp.float32)
    visible = key_pos[None, None, :] <= positions[None, :, None]
    scores = jnp.where(visible, scores, -1e30)
    row_max = jnp.max(scores, axis=-1, keepdims=True)
    exponent = jnp.exp(scores - row_max)
    weights = (exponent / jnp.sum(exponent, axis=-1, keepdims=True)).astype(jnp.bfloat16)
    attended = jnp.einsum("hrc,cd->rhd", weights, value_rows, preferred_element_type=jnp.float32)
    return attended.reshape(1, rec_count, heads_here * HD).astype(jnp.bfloat16)


CORE, XBIT, YBIT = 1, 2, 4


def flip(bit, count):
    return [(s, s ^ bit) for s in range(count)]


def norm_kernel(states_ref, keep_ref, send_ref):
    me = lax.axis_index("store")
    width = states_ref.shape[1]
    depth = width // 8
    total = jnp.zeros((states_ref.shape[0], 1), F32)
    for s in range(8):
        part = states_ref[:, s * depth : (s + 1) * depth].astype(F32)
        total += jnp.sum(part * part, axis=1, keepdims=True)
    scale = lax.rsqrt(total / width + 1e-05)
    for r in range(4):
        for core, out in ((0, keep_ref), (1, send_ref)):
            s = lax.bitwise_xor(me, r * 2 + core)
            part = states_ref[:, pl.ds(pl.multiple_of(s * depth, depth), depth)].astype(F32)
            out[:, r * depth : (r + 1) * depth] = (part * scale).astype(BF16)


def norm_split(states):
    rows, width = states.shape
    half = jax.ShapeDtypeStruct((rows, width // 2), BF16)
    return pl.pallas_call(
        norm_kernel,
        out_shape=(half, half),
        compiler_params=pltpu.CompilerParams(vmem_limit_bytes=16 << 20),
        cost_estimate=TINY,
        name="norm_split",
    )(states)


def cut_kernel(plan, n_in, *refs):
    outs, sems = refs[n_in:-1], refs[-1]
    copies = []
    for out, pieces in zip(outs, plan):
        for source, (row, col), (to_row, to_col), (rows, cols) in pieces:
            copies.append(
                pltpu.make_async_copy(
                    refs[source].at[pl.ds(row, rows), pl.ds(col, cols)],
                    out.at[pl.ds(to_row, rows), pl.ds(to_col, cols)],
                    sems.at[len(copies)],
                )
            )
    for copy in copies:
        copy.start()
    for copy in copies:
        copy.wait()


def cut(sources, plan, shapes, gates=(), near=False, limit=58):
    gates = jax.tree.leaves(gates)
    args = [*sources, *gates]
    hbm = pl.BlockSpec(memory_space=pltpu.HBM)
    vmem = pl.BlockSpec(memory_space=pltpu.VMEM)
    anywhere = pl.BlockSpec(memory_space=pl.ANY)
    return pl.pallas_call(
        functools.partial(cut_kernel, plan, len(args)),
        in_specs=[vmem if near else hbm] * len(sources) + [anywhere] * len(gates),
        out_specs=[hbm if near else vmem] * len(shapes),
        out_shape=[jax.ShapeDtypeStruct(shape, BF16) for shape in shapes],
        scratch_shapes=[pltpu.SemaphoreType.DMA((sum(len(p) for p in plan),))],
        compiler_params=pltpu.CompilerParams(vmem_limit_bytes=limit << 20),
        cost_estimate=TINY,
        name="cut",
    )(*args)


def relay_kernel(own, two, *refs):
    up, down, sems = refs[-3:]
    me = lax.axis_index("ctx")

    def moves(act):
        for way, out in enumerate((up, down)):
            for source, chosen in ((own, me == 1 + way), (two, me != 1 + way)):

                @pl.when(chosen)
                def _():
                    act(pltpu.make_async_copy(source, out, sems.at[way]))

    moves(lambda c: c.start())
    moves(lambda c: c.wait())


def relay(own, two, gates):
    hbm = pl.BlockSpec(memory_space=pltpu.HBM)
    out = jax.ShapeDtypeStruct(own.shape, BF16)
    return pl.pallas_call(
        relay_kernel,
        in_specs=[hbm] * 2 + [pl.BlockSpec(memory_space=pl.ANY)] * len(gates),
        out_shape=(out, out),
        scratch_shapes=[pltpu.SemaphoreType.DMA((2,))],
        compiler_params=pltpu.CompilerParams(vmem_limit_bytes=4 << 20),
        cost_estimate=TINY,
        name="relay",
    )(own, two, *gates)


def sort_kernel(blocks_ref, places_ref, *refs):
    out_ref = refs[-1]
    heads = out_ref.shape[0]
    size = blocks_ref.shape[1]
    for j in range(places_ref.shape[0]):
        block = blocks_ref[places_ref[j]]
        for h in range(heads):
            rows = slice(j * size, (j + 1) * size)
            out_ref[h, rows, :HD] = block[:, h * HD : (h + 1) * HD]
            out_ref[h, rows, HD:] = block[:, (heads + h) * HD : (heads + h + 1) * HD]


def sort_blocks(blocks, places, gates):
    anywhere = pl.BlockSpec(memory_space=pl.ANY)
    count, size, _ = blocks.shape
    return pl.pallas_call(
        sort_kernel,
        in_specs=[pl.BlockSpec(memory_space=pltpu.VMEM), pl.BlockSpec(memory_space=pltpu.SMEM)]
        + [anywhere] * len(gates),
        out_shape=jax.ShapeDtypeStruct((KVH, places.shape[0] * size, 2 * HD), BF16),
        compiler_params=pltpu.CompilerParams(vmem_limit_bytes=4 << 20),
        cost_estimate=TINY,
        name="sort_blocks",
    )(blocks, places, *gates)


STEP = 2 * HD


def share(total, shards, own, sib, cols):
    rows = own.shape[0] // shards
    for z in range(shards):
        here = slice(z * rows, (z + 1) * rows)
        own[here, cols] = total[2 * z * rows : (2 * z + 1) * rows]
        sib[here, cols] = total[(2 * z + 1) * rows : (2 * z + 2) * rows]


def load_rows_kernel(*refs):
    parts, out_ref, sems = refs[:5], refs[-2], refs[-1]
    me = lax.axis_index("ctx")
    rows = parts[0].shape[0]

    def copies(act):
        for k in range(4):
            start = pl.multiple_of(lax.bitwise_xor(me, k) * rows, rows)
            target = out_ref.at[pl.ds(start, rows)]
            if k < 3:
                act(pltpu.make_async_copy(parts[k], target, sems.at[k]))
            else:
                for source, chosen in ((parts[3], me >= 2), (parts[4], me < 2)):

                    @pl.when(chosen)
                    def _():
                        act(pltpu.make_async_copy(source, target, sems.at[k]))

    copies(lambda c: c.start())
    copies(lambda c: c.wait())


def load_rows(parts, gate):
    rows, width = parts[0].shape
    return pl.pallas_call(
        load_rows_kernel,
        in_specs=[pl.BlockSpec(memory_space=pltpu.HBM)] * 5 + [pl.BlockSpec(memory_space=pl.ANY)],
        out_shape=jax.ShapeDtypeStruct((4 * rows, width), BF16),
        scratch_shapes=[pltpu.SemaphoreType.DMA((4,))],
        compiler_params=pltpu.CompilerParams(vmem_limit_bytes=12 << 20),
        cost_estimate=TINY,
        name="load_rows",
    )(*parts, gate)


def load_weights_kernel(kv, q, first_x, first_y, last_x, last_y, out_ref, token, sems):
    depth = kv.shape[0]
    copies = []
    for r, sources in enumerate(((kv, q), (first_x, last_x), (first_y, last_y))):
        col = 0
        for source in sources:
            width = source.shape[1]
            target = out_ref.at[pl.ds(r * depth, depth), pl.ds(col, width)]
            copies.append(pltpu.make_async_copy(source, target, sems.at[len(copies)]))
            col += width
    for copy in copies:
        copy.start()
    token[...] = jnp.zeros(token.shape, F32)
    for copy in copies:
        copy.wait()


def load_weights(*parts):
    depth = parts[0].shape[0]
    cols = parts[0].shape[1] + parts[1].shape[1]
    return pl.pallas_call(
        load_weights_kernel,
        in_specs=[pl.BlockSpec(memory_space=pltpu.HBM)] * 6,
        out_shape=(
            jax.ShapeDtypeStruct((3 * depth, cols), BF16),
            jax.ShapeDtypeStruct((8, HD), F32),
        ),
        scratch_shapes=[pltpu.SemaphoreType.DMA((6,))],
        compiler_params=pltpu.CompilerParams(vmem_limit_bytes=16 << 20),
        cost_estimate=TINY,
        name="load_weights",
    )(*parts)


def gather_kernel(asked_ref, store_ref, *refs):
    out_ref, sems = refs[-2:]
    count = asked_ref.shape[0]
    copies = [
        pltpu.make_async_copy(store_ref.at[asked_ref[i]], out_ref.at[i], sems.at[i])
        for i in range(count)
    ]
    for copy in copies:
        copy.start()
    for copy in copies:
        copy.wait()


def gather_blocks(asked, store_kv, gate):
    return pl.pallas_call(
        gather_kernel,
        in_specs=[
            pl.BlockSpec(memory_space=pltpu.SMEM),
            pl.BlockSpec(memory_space=pltpu.HBM),
            pl.BlockSpec(memory_space=pl.ANY),
        ],
        out_shape=jax.ShapeDtypeStruct(asked.shape + store_kv.shape[1:], BF16),
        scratch_shapes=[pltpu.SemaphoreType.DMA(asked.shape)],
        compiler_params=pltpu.CompilerParams(vmem_limit_bytes=4 << 20),
        cost_estimate=TINY,
        name="gather_blocks",
    )(asked, store_kv, gate)


def multiply(a_ref, w_ref, d_x, d_y, col, near):
    depth = w_ref.shape[0] // 3
    total = 0.0
    for r in range(3):
        total += jnp.dot(
            a_ref[:, r * depth : (r + 1) * depth],
            w_ref[r * depth : (r + 1) * depth, col : col + STEP],
            preferred_element_type=F32,
        )
    if d_x is None:
        return total
    return total + diagonal_part(a_ref, d_x, d_y, near)


def diagonal_part(a_ref, d_x, d_y, near):
    h = d_x.shape[0]
    part = jnp.dot(a_ref[:, 6 * h : 7 * h], d_x[:, near : near + STEP], preferred_element_type=F32)
    return part + jnp.dot(a_ref[:, 7 * h :], d_y[:, near : near + STEP], preferred_element_type=F32)


def project_kv_kernel(a_ref, w_ref, d_x, d_y, own, sib):
    share(multiply(a_ref, w_ref, d_x, d_y, 0, 0), 4, own, sib, slice(0, STEP))


def project_q_kernel(kv_cols, a_ref, w_ref, d_x, d_y, *refs):
    own, sib, rest = refs[-3:]
    early = own.shape[1]
    for col in range(0, early, STEP):
        total = multiply(a_ref, w_ref, d_x, d_y, kv_cols + col, kv_cols + col)
        share(total, 4, own, sib, slice(col, col + STEP))
    for col in range(0, rest.shape[1], STEP):
        rest[:, col : col + STEP] = multiply(a_ref, w_ref, None, None, kv_cols + early + col, 0)


def project_last_kernel(a_ref, d_x, d_y, rest, *refs):
    own, sib = refs[-2:]
    for col in range(0, rest.shape[1], STEP):
        total = rest[:, col : col + STEP] + diagonal_part(a_ref, d_x, d_y, col)
        share(total, 4, own, sib, slice(col, col + STEP))


def project(kernel, near, gates, outs, limit, work):
    vmem = pl.BlockSpec(memory_space=pltpu.VMEM)
    return pl.pallas_call(
        kernel,
        in_specs=[vmem] * len(near) + [pl.BlockSpec(memory_space=pl.ANY)] * len(gates),
        out_shape=[jax.ShapeDtypeStruct(shape, F32) for shape in outs],
        compiler_params=pltpu.CompilerParams(vmem_limit_bytes=limit << 20),
        cost_estimate=TINY,
        name="project",
    )(*near, *gates)


def fresh_kernel(own, sib, fresh_ref, first_ref, second_ref):
    me = lax.axis_index("ctx")
    fresh = own[...] + sib[...]
    low, high = fresh[:, :HD], fresh[:, HD:]
    fresh_ref[...] = fresh.astype(BF16)
    first_ref[...] = jnp.where(me == 0, high, low).astype(BF16)
    second_ref[...] = jnp.where(me == 3, low, high).astype(BF16)


def make_fresh(own, sib):
    rows = own.shape[0]
    out = lambda cols: jax.ShapeDtypeStruct((rows, cols), BF16)
    return pl.pallas_call(
        fresh_kernel,
        out_shape=(out(2 * HD), out(HD), out(HD)),
        compiler_params=pltpu.CompilerParams(vmem_limit_bytes=4 << 20),
        cost_estimate=TINY,
        name="fresh",
    )(own, sib)


def turn(values, cosine, sine):
    return values * cosine + pltpu.roll(values, HD // 2, 1) * sine


def assemble_kernel(fresh_ref, first_ref, second_ref, cached_ref, cos_ref, sin_ref, target_ref, key_ref, value_ref):
    me = lax.axis_index("ctx")
    low, high = fresh_ref[:, :HD].astype(F32), fresh_ref[:, HD:].astype(F32)
    first, second = first_ref[...].astype(F32), second_ref[...].astype(F32)
    fresh_key = jnp.where(me == 0, low, jnp.where(me == 3, second, first))
    fresh_value = jnp.where(me == 0, first, jnp.where(me == 3, high, second)).astype(BF16)
    fresh_key = turn(fresh_key, cos_ref[...], sin_ref[...]).astype(BF16)
    context = cached_ref.shape[0]
    count = fresh_key.shape[0]
    hit = lax.broadcasted_iota(jnp.int32, (context, count), 0) == target_ref[...]
    pick = jnp.where(hit, 1.0, 0.0)
    taken = jnp.max(pick, axis=1, keepdims=True) > 0.5
    pick = pick.astype(BF16)
    key_new = jnp.dot(pick, fresh_key, preferred_element_type=F32).astype(BF16)
    value_new = jnp.dot(pick, fresh_value, preferred_element_type=F32).astype(BF16)
    key_ref[...] = jnp.where(taken, key_new, cached_ref[:, :HD])
    value_ref[...] = jnp.where(taken, value_new, cached_ref[:, HD:]).T


def assemble(fresh, first, second, cached, cosine, sine, targets):
    context = cached.shape[0]
    return pl.pallas_call(
        assemble_kernel,
        out_shape=(
            jax.ShapeDtypeStruct((context, HD), BF16),
            jax.ShapeDtypeStruct((HD, context), BF16),
        ),
        compiler_params=pltpu.CompilerParams(vmem_limit_bytes=16 << 20),
        cost_estimate=TINY,
        name="assemble",
    )(fresh, first, second, cached, cosine, sine, targets)


def attend_kernel(heads, *refs):
    own_ref, sib_ref, key_ref, value_ref, cos_ref, sin_ref, pos_ref, key_pos_ref, *rest = refs
    out_ref = rest[-1]
    visible = key_pos_ref[...] <= pos_ref[...]
    for h in range(heads):
        cols = slice(h * HD, (h + 1) * HD)
        raw = own_ref[:, cols] + sib_ref[:, cols]
        query = (turn(raw, cos_ref[...], sin_ref[...]) * HD ** (-0.5)).astype(BF16)
        scores = lax.dot_general(
            key_ref[...], query, (((1,), (1,)), ((), ())), preferred_element_type=F32
        )
        scores = jnp.where(visible, scores, -1e30)
        exponent = jnp.exp(scores - jnp.max(scores, axis=0, keepdims=True))
        weights = exponent * (1.0 / jnp.sum(exponent, axis=0, keepdims=True))
        turned = jnp.dot(value_ref[...], weights.astype(BF16), preferred_element_type=F32)
        out_ref[:, cols] = turned.T.astype(BF16)


def attend(own, sib, shared, width, start, before):
    rec_count, cols = own.shape
    args = [own, sib, *shared]
    specs = [pl.BlockSpec(a.shape, lambda i: (0, 0)) for a in args]
    aliases = {}
    if before is not None:
        aliases = {len(args): 0}
        args.append(before)
        specs.append(pl.BlockSpec(memory_space=pltpu.HBM))
    return pl.pallas_call(
        functools.partial(attend_kernel, cols // HD),
        grid=(1,),
        in_specs=specs,
        out_specs=pl.BlockSpec((rec_count, cols), lambda i: (0, start // cols)),
        out_shape=jax.ShapeDtypeStruct((rec_count, width), BF16),
        input_output_aliases=aliases,
        compiler_params=pltpu.CompilerParams(vmem_limit_bytes=16 << 20),
        cost_estimate=TINY,
        name="attend",
    )(*args)


def fast_body(store_kv, block_slot, block_owner, rec_pos, states, w_query, w_keyval):
    store_count = lax.axis_size("store")
    ctx_count = lax.axis_size("ctx")
    my_index = lax.axis_index("ctx")
    piece_rows = store_kv.shape[1]
    block_count = block_slot.shape[1]
    rec_count = rec_pos.shape[1]
    query_cols = w_query.shape[1]
    depth = w_query.shape[0]
    positions = rec_pos[0]
    xf, yf, cf = (flip(b, store_count) for b in (XBIT, YBIT, CORE))
    by_x = lambda a: lax.ppermute(a, "store", xf)
    by_y = lambda a: lax.ppermute(a, "store", yf)
    by_core = lambda a: lax.ppermute(a, "store", cf)

    along = lambda a, pairs: lax.ppermute(a, "ctx", pairs)
    kv_cols = w_keyval.shape[1]
    late = query_cols // 2
    early = query_cols - late
    first_cols = kv_cols + early
    half = depth // 2

    asked, places = swap_ids(block_slot[0], block_owner[0], store_count)
    (w_first,) = cut(
        (w_keyval, w_query),
        [[(0, (0, 0), (0, 0), (depth, kv_cols)), (1, (0, 0), (0, kv_cols), (depth, early))]],
        [(depth, first_cols)],
        (asked,),
    )
    first_x, first_y = by_x(w_first), by_y(w_first)
    gathered = gather_blocks(asked.reshape(-1), store_kv, w_first)
    arrived = lax.all_to_all(gathered, "store", split_axis=0, concat_axis=0, tiled=True)
    (w_last,) = cut(
        (w_query,), [[(0, (0, early), (0, 0), (depth, late))]], [(depth, late)], (arrived, first_x, first_y)
    )
    last_x, last_y = by_x(w_last), by_y(w_last)
    by_head = sort_blocks(arrived, places, (w_last,))
    cached = lax.all_to_all(by_head, "ctx", split_axis=0, concat_axis=0, tiled=True)
    cached = cached.reshape(-1, 2 * HD)

    keep, send = norm_split(states[0])
    shard, width = keep.shape
    (both,) = cut(
        (keep, by_core(send)),
        [[(0, (0, 0), (0, 0), (shard, width)), (1, (0, 0), (shard, 0), (shard, width))]],
        [(2 * shard, width)],
        near=True,
    )
    along = lambda a, pairs: lax.ppermute(a, "ctx", pairs)
    two = along(both, [(0, 2), (1, 3), (2, 0), (3, 1)])
    one = along(both, [(0, 1), (1, 0), (2, 3), (3, 2)])
    up, down = relay(both, two, (one, cached))
    shard_parts = (
        both,
        one,
        two,
        along(up, [(1, 2), (2, 3)]),
        along(down, [(2, 1), (1, 0)]),
    )

    def diagonal(from_x, from_y, gates, limit):
        cols = from_x.shape[1]
        sent = cut(
            (from_y, from_x),
            [[(0, (0, 0), (0, 0), (half, cols))], [(1, (half, 0), (0, 0), (half, cols))]],
            [(half, cols)] * 2,
            gates,
            limit=limit,
        )
        return (by_x(sent[0]), by_y(sent[1])), sent[0]

    diag_first, _ = diagonal(first_x, first_y, (up, last_x, last_y), 8)
    weights, loaded = load_weights(w_keyval, w_query, first_x, first_y, last_x, last_y)
    diag_last, sent_last = diagonal(last_x, last_y, (loaded,), 6)

    shard_rows = block_count * piece_rows
    frequency = jnp.exp(
        jnp.arange(HD // 2, dtype=F32) * (-2.0 * math.log(500000.0) / HD)
    )
    angles = positions.astype(F32)[:, None] * frequency[None, :]
    cos_half, sin_half = jnp.cos(angles), jnp.sin(angles)
    cosine = jnp.concatenate((cos_half, cos_half), axis=1)
    sine = jnp.concatenate((-sin_half, sin_half), axis=1)
    block_len = piece_rows * ctx_count
    targets = (
        positions % block_len // piece_rows * shard_rows
        + positions // block_len * piece_rows
        + positions % piece_rows
    )

    row_ids = jnp.arange(ctx_count * shard_rows)
    key_pos = (
        row_ids % shard_rows // piece_rows * block_len
        + row_ids // shard_rows * piece_rows
        + row_ids % piece_rows
    )

    rows = load_rows(shard_parts, sent_last)
    kv_own, kv_sib = project(
        project_kv_kernel,
        (rows, weights, *diag_first),
        (),
        [(rec_count, kv_cols)] * 2,
        20,
        2 * rows.size * kv_cols,
    )
    fresh, to_first, to_second = make_fresh(kv_own, by_core(kv_sib))
    first = along(to_first, [(0, 1), (1, 2), (2, 0)])
    second = along(to_second, [(1, 3), (2, 1), (3, 2)])
    early_own, early_sib, rest = project(
        functools.partial(project_q_kernel, kv_cols),
        (rows, weights, *diag_first),
        (to_first,),
        [(rec_count, early)] * 2 + [(2 * rec_count, late)],
        22,
        2 * rows.size * query_cols,
    )
    key_rows, value_rows = assemble(
        fresh, first, second, cached, cosine, sine, targets.reshape(1, rec_count)
    )
    shared = (
        key_rows,
        value_rows,
        cosine,
        sine,
        positions.reshape(1, rec_count),
        key_pos.reshape(-1, 1),
    )
    result = attend(early_own, by_core(early_sib), shared, query_cols, 0, None)
    own, sib = project(
        project_last_kernel,
        (rows, *diag_last, rest),
        (first, second, cached),
        [(rec_count, late)] * 2,
        12,
        rows.size * late // 2,
    )
    result = attend(own, by_core(sib), shared, query_cols, early, result)
    return result.reshape(1, rec_count, query_cols)


def solution(mesh):
    fast = mesh.shape["store"] == 8 and mesh.shape["ctx"] == KVH
    return jax.shard_map(
        fast_body if fast else general_body,
        mesh=mesh,
        in_specs=(
            P("store", "ctx", None),
            P("store", None),
            P("store", None),
            P("store", None),
            P("store", "ctx", None),
            P("store", "ctx"),
            P("store", "ctx"),
        ),
        out_specs=P("store", None, "ctx"),
        check_vma=False,
    )
```

```python
import functools
import math

import jax
import jax.numpy as jnp
from jax import lax
from jax.experimental import pallas as pl
from jax.experimental.pallas import tpu as pltpu
from jax.sharding import PartitionSpec as P

QH = 32
KVH = 4
HD = 128
CAP = 2
F32 = jnp.float32
BF16 = jnp.bfloat16
TINY = pl.CostEstimate(flops=1, bytes_accessed=1, transcendentals=0)


def rotate(values, positions):
    midpoint = values.shape[-1] // 2
    frequency = jnp.exp(
        jnp.arange(midpoint, dtype=jnp.float32) * (-2.0 * math.log(500000.0) / values.shape[-1])
    )
    angles = positions.astype(jnp.float32)[:, None] * frequency[None, :]
    cosine = jnp.cos(angles)[:, None, :]
    sine_term = jnp.sin(angles)[:, None, :]
    leading = values[..., :midpoint]
    trailing = values[..., midpoint:]
    return jnp.concatenate(
        (leading * cosine - trailing * sine_term, trailing * cosine + leading * sine_term), axis=-1
    )


def normalize(states):
    floated = states.astype(jnp.float32)
    return (
        floated * lax.rsqrt(jnp.mean(floated * floated, axis=-1, keepdims=True) + 1e-05)
    ).astype(jnp.bfloat16)


def swap_ids(slot_ids, owners, store_count):
    block_count = slot_ids.shape[0]
    slot_order = jnp.arange(block_count)
    earlier = slot_order[None, :] < slot_order[:, None]
    slot_ranks = jnp.sum((owners[:, None] == owners[None, :]) & earlier, axis=1)
    slot_hits = (owners[:, None, None] == jnp.arange(store_count)[None, :, None]) & (
        slot_ranks[:, None, None] == jnp.arange(CAP)[None, None, :]
    )
    wanted = jnp.sum(jnp.where(slot_hits, slot_ids[:, None, None], 0), axis=0)
    asked = lax.all_to_all(wanted, "store", split_axis=0, concat_axis=0, tiled=True)
    return asked, owners * CAP + slot_ranks


def fetch_blocks(store_kv, asked, places):
    arrived = lax.all_to_all(store_kv[asked], "store", split_axis=0, concat_axis=0, tiled=True)
    return arrived.reshape((-1,) + store_kv.shape[1:])[places].reshape(-1, store_kv.shape[2])


def general_body(store_kv, block_slot, block_owner, rec_pos, states, w_query, w_keyval):
    ctx_count = lax.axis_size("ctx")
    my_index = lax.axis_index("ctx")
    piece_rows = store_kv.shape[1]
    block_count = block_slot.shape[1]
    rec_count = rec_pos.shape[1]
    positions = rec_pos[0]
    shard_rows = block_count * piece_rows
    local_rows = fetch_blocks(
        store_kv, *swap_ids(block_slot[0], block_owner[0], lax.axis_size("store"))
    )
    normed = normalize(states[0])
    query_cols = w_query.shape[1]
    query_weight, keyval_weight = (
        lax.all_gather(w_query, "store", axis=0, tiled=True),
        lax.all_gather(w_keyval, "store", axis=0, tiled=True),
    )
    row_piece = lax.all_gather(normed, "ctx", axis=0, tiled=True)
    query_raw = jnp.dot(row_piece, query_weight, preferred_element_type=jnp.float32)
    keyval_raw = jnp.dot(row_piece, keyval_weight, preferred_element_type=jnp.float32)
    heads_here = query_cols // HD
    group_size = QH // KVH
    queries = (
        rotate(query_raw.reshape(rec_count, heads_here, HD), positions) * HD ** (-0.5)
    ).astype(jnp.bfloat16)
    fresh_rows = lax.all_gather(keyval_raw.astype(jnp.bfloat16), "ctx", axis=1, tiled=True)
    shared_head = my_index * heads_here // group_size
    fresh_key = rotate(
        lax.dynamic_slice_in_dim(fresh_rows, shared_head * HD, HD, 1)
        .astype(jnp.float32)
        .reshape(rec_count, 1, HD),
        positions,
    )
    fresh_key = fresh_key.astype(jnp.bfloat16).reshape(rec_count, HD)
    fresh_value = lax.dynamic_slice_in_dim(fresh_rows, KVH * HD + shared_head * HD, HD, 1)
    gathered = lax.all_gather(local_rows, "ctx", axis=0, tiled=True)
    key_rows = lax.dynamic_slice_in_dim(gathered, shared_head * HD, HD, 1)
    value_rows = lax.dynamic_slice_in_dim(gathered, KVH * HD + shared_head * HD, HD, 1)
    row_ids = jnp.arange(ctx_count * shard_rows)
    block_len = piece_rows * ctx_count
    key_pos = (
        row_ids % shard_rows // piece_rows * block_len
        + row_ids // shard_rows * piece_rows
        + row_ids % piece_rows
    )
    targets = (
        positions % block_len // piece_rows * shard_rows
        + positions // block_len * piece_rows
        + positions % piece_rows
    )
    key_rows = key_rows.at[targets].set(fresh_key)
    value_rows = value_rows.at[targets].set(fresh_value)
    scores = jnp.einsum("rhd,cd->hrc", queries, key_rows, preferred_element_type=jnp.float32)
    visible = key_pos[None, None, :] <= positions[None, :, None]
    scores = jnp.where(visible, scores, -1e30)
    row_max = jnp.max(scores, axis=-1, keepdims=True)
    exponent = jnp.exp(scores - row_max)
    weights = (exponent / jnp.sum(exponent, axis=-1, keepdims=True)).astype(jnp.bfloat16)
    attended = jnp.einsum("hrc,cd->rhd", weights, value_rows, preferred_element_type=jnp.float32)
    return attended.reshape(1, rec_count, heads_here * HD).astype(jnp.bfloat16)


CORE, XBIT, YBIT = 1, 2, 4


def flip(bit, count):
    return [(s, s ^ bit) for s in range(count)]


def norm_kernel(states_ref, keep_ref, send_ref):
    me = lax.axis_index("store")
    width = states_ref.shape[1]
    depth = width // 8
    total = jnp.zeros((states_ref.shape[0], 1), F32)
    for s in range(8):
        part = states_ref[:, s * depth : (s + 1) * depth].astype(F32)
        total += jnp.sum(part * part, axis=1, keepdims=True)
    scale = lax.rsqrt(total / width + 1e-05)
    for r in range(4):
        for core, out in ((0, keep_ref), (1, send_ref)):
            s = lax.bitwise_xor(me, r * 2 + core)
            part = states_ref[:, pl.ds(pl.multiple_of(s * depth, depth), depth)].astype(F32)
            out[:, r * depth : (r + 1) * depth] = (part * scale).astype(BF16)


def norm_split(states):
    rows, width = states.shape
    half = jax.ShapeDtypeStruct((rows, width // 2), BF16)
    return pl.pallas_call(
        norm_kernel,
        out_shape=(half, half),
        compiler_params=pltpu.CompilerParams(vmem_limit_bytes=16 << 20),
        cost_estimate=TINY,
        name="norm_split",
    )(states)


def cut_kernel(plan, n_in, *refs):
    outs, sems = refs[n_in:-1], refs[-1]
    copies = []
    for out, pieces in zip(outs, plan):
        for source, (row, col), (to_row, to_col), (rows, cols) in pieces:
            copies.append(
                pltpu.make_async_copy(
                    refs[source].at[pl.ds(row, rows), pl.ds(col, cols)],
                    out.at[pl.ds(to_row, rows), pl.ds(to_col, cols)],
                    sems.at[len(copies)],
                )
            )
    for copy in copies:
        copy.start()
    for copy in copies:
        copy.wait()


def cut(sources, plan, shapes, gates=(), near=False, limit=58):
    gates = jax.tree.leaves(gates)
    args = [*sources, *gates]
    hbm = pl.BlockSpec(memory_space=pltpu.HBM)
    vmem = pl.BlockSpec(memory_space=pltpu.VMEM)
    anywhere = pl.BlockSpec(memory_space=pl.ANY)
    return pl.pallas_call(
        functools.partial(cut_kernel, plan, len(args)),
        in_specs=[vmem if near else hbm] * len(sources) + [anywhere] * len(gates),
        out_specs=[hbm if near else vmem] * len(shapes),
        out_shape=[jax.ShapeDtypeStruct(shape, BF16) for shape in shapes],
        scratch_shapes=[pltpu.SemaphoreType.DMA((sum(len(p) for p in plan),))],
        compiler_params=pltpu.CompilerParams(vmem_limit_bytes=limit << 20),
        cost_estimate=TINY,
        name="cut",
    )(*args)


def relay_kernel(own, two, *refs):
    up, down, sems = refs[-3:]
    me = lax.axis_index("ctx")

    def moves(act):
        for way, out in enumerate((up, down)):
            for source, chosen in ((own, me == 1 + way), (two, me != 1 + way)):

                @pl.when(chosen)
                def _():
                    act(pltpu.make_async_copy(source, out, sems.at[way]))

    moves(lambda c: c.start())
    moves(lambda c: c.wait())


def relay(own, two, gates):
    hbm = pl.BlockSpec(memory_space=pltpu.HBM)
    out = jax.ShapeDtypeStruct(own.shape, BF16)
    return pl.pallas_call(
        relay_kernel,
        in_specs=[hbm] * 2 + [pl.BlockSpec(memory_space=pl.ANY)] * len(gates),
        out_shape=(out, out),
        scratch_shapes=[pltpu.SemaphoreType.DMA((2,))],
        compiler_params=pltpu.CompilerParams(vmem_limit_bytes=4 << 20),
        cost_estimate=TINY,
        name="relay",
    )(own, two, *gates)


def sort_kernel(blocks_ref, places_ref, *refs):
    out_ref = refs[-1]
    heads = out_ref.shape[0]
    size = blocks_ref.shape[1]
    for j in range(places_ref.shape[0]):
        block = blocks_ref[places_ref[j]]
        for h in range(heads):
            rows = slice(j * size, (j + 1) * size)
            out_ref[h, rows, :HD] = block[:, h * HD : (h + 1) * HD]
            out_ref[h, rows, HD:] = block[:, (heads + h) * HD : (heads + h + 1) * HD]


def sort_blocks(blocks, places, gates):
    anywhere = pl.BlockSpec(memory_space=pl.ANY)
    count, size, _ = blocks.shape
    return pl.pallas_call(
        sort_kernel,
        in_specs=[pl.BlockSpec(memory_space=pltpu.VMEM), pl.BlockSpec(memory_space=pltpu.SMEM)]
        + [anywhere] * len(gates),
        out_shape=jax.ShapeDtypeStruct((KVH, places.shape[0] * size, 2 * HD), BF16),
        compiler_params=pltpu.CompilerParams(vmem_limit_bytes=4 << 20),
        cost_estimate=TINY,
        name="sort_blocks",
    )(blocks, places, *gates)


STEP = 2 * HD


def share(total, shards, own, sib, cols):
    rows = own.shape[0] // shards
    for z in range(shards):
        here = slice(z * rows, (z + 1) * rows)
        own[here, cols] = total[2 * z * rows : (2 * z + 1) * rows]
        sib[here, cols] = total[(2 * z + 1) * rows : (2 * z + 2) * rows]


def load_rows_kernel(*refs):
    parts, out_ref, sems = refs[:5], refs[-2], refs[-1]
    me = lax.axis_index("ctx")
    rows = parts[0].shape[0]

    def copies(act):
        for k in range(4):
            start = pl.multiple_of(lax.bitwise_xor(me, k) * rows, rows)
            target = out_ref.at[pl.ds(start, rows)]
            if k < 3:
                act(pltpu.make_async_copy(parts[k], target, sems.at[k]))
            else:
                for source, chosen in ((parts[3], me >= 2), (parts[4], me < 2)):

                    @pl.when(chosen)
                    def _():
                        act(pltpu.make_async_copy(source, target, sems.at[k]))

    copies(lambda c: c.start())
    copies(lambda c: c.wait())


def load_rows(parts, gate):
    rows, width = parts[0].shape
    return pl.pallas_call(
        load_rows_kernel,
        in_specs=[pl.BlockSpec(memory_space=pltpu.HBM)] * 5 + [pl.BlockSpec(memory_space=pl.ANY)],
        out_shape=jax.ShapeDtypeStruct((4 * rows, width), BF16),
        scratch_shapes=[pltpu.SemaphoreType.DMA((4,))],
        compiler_params=pltpu.CompilerParams(vmem_limit_bytes=12 << 20),
        cost_estimate=TINY,
        name="load_rows",
    )(*parts, gate)


def load_weights_kernel(kv, q, first_x, first_y, last_x, last_y, out_ref, token, sems):
    depth = kv.shape[0]
    copies = []
    for r, sources in enumerate(((kv, q), (first_x, last_x), (first_y, last_y))):
        col = 0
        for source in sources:
            width = source.shape[1]
            target = out_ref.at[pl.ds(r * depth, depth), pl.ds(col, width)]
            copies.append(pltpu.make_async_copy(source, target, sems.at[len(copies)]))
            col += width
    for copy in copies:
        copy.start()
    token[...] = jnp.zeros(token.shape, F32)
    for copy in copies:
        copy.wait()


def load_weights(*parts):
    depth = parts[0].shape[0]
    cols = parts[0].shape[1] + parts[1].shape[1]
    return pl.pallas_call(
        load_weights_kernel,
        in_specs=[pl.BlockSpec(memory_space=pltpu.HBM)] * 6,
        out_shape=(
            jax.ShapeDtypeStruct((3 * depth, cols), BF16),
            jax.ShapeDtypeStruct((8, HD), F32),
        ),
        scratch_shapes=[pltpu.SemaphoreType.DMA((6,))],
        compiler_params=pltpu.CompilerParams(vmem_limit_bytes=16 << 20),
        cost_estimate=TINY,
        name="load_weights",
    )(*parts)


def gather_kernel(asked_ref, store_ref, *refs):
    out_ref, sems = refs[-2:]
    owners, cap = asked_ref.shape
    copies = [
        pltpu.make_async_copy(
            store_ref.at[asked_ref[i, j]], out_ref.at[i * cap + j], sems.at[i * cap + j]
        )
        for i in range(owners)
        for j in range(cap)
    ]
    for copy in copies:
        copy.start()
    for copy in copies:
        copy.wait()


def gather_blocks(asked, store_kv, gate):
    return pl.pallas_call(
        gather_kernel,
        in_specs=[
            pl.BlockSpec(memory_space=pltpu.SMEM),
            pl.BlockSpec(memory_space=pltpu.HBM),
            pl.BlockSpec(memory_space=pl.ANY),
        ],
        out_shape=jax.ShapeDtypeStruct((asked.size,) + store_kv.shape[1:], BF16),
        scratch_shapes=[pltpu.SemaphoreType.DMA((asked.size,))],
        compiler_params=pltpu.CompilerParams(vmem_limit_bytes=4 << 20),
        cost_estimate=TINY,
        name="gather_blocks",
    )(asked, store_kv, gate)


def diagonal_part(a_ref, d_x, d_y, col):
    h = d_x.shape[0]
    part = jnp.dot(a_ref[:, 6 * h : 7 * h], d_x[:, col : col + STEP], preferred_element_type=F32)
    return part + jnp.dot(a_ref[:, 7 * h :], d_y[:, col : col + STEP], preferred_element_type=F32)


def project_near_kernel(a_ref, w_ref, first, last):
    depth = w_ref.shape[0] // 3
    col = 0
    for out in (first, last):
        for here in range(0, out.shape[1], STEP):
            total = 0.0
            for r in range(3):
                part = slice(r * depth, (r + 1) * depth)
                total += jnp.dot(
                    a_ref[:, part], w_ref[part, col : col + STEP], preferred_element_type=F32
                )
            out[:, here : here + STEP] = total
            col += STEP


def project_first_kernel(a_ref, d_x, d_y, rest, kv_own, kv_sib, own, sib):
    for col in range(0, rest.shape[1], STEP):
        total = rest[:, col : col + STEP] + diagonal_part(a_ref, d_x, d_y, col)
        if col == 0:
            share(total, 4, kv_own, kv_sib, slice(0, STEP))
        else:
            share(total, 4, own, sib, slice(col - STEP, col))


def project_last_kernel(a_ref, d_x, d_y, rest, *refs):
    own, sib = refs[-2:]
    for col in range(0, rest.shape[1], STEP):
        total = rest[:, col : col + STEP] + diagonal_part(a_ref, d_x, d_y, col)
        share(total, 4, own, sib, slice(col, col + STEP))


def project(kernel, near, gates, outs, limit):
    vmem = pl.BlockSpec(memory_space=pltpu.VMEM)
    return pl.pallas_call(
        kernel,
        in_specs=[vmem] * len(near) + [pl.BlockSpec(memory_space=pl.ANY)] * len(gates),
        out_shape=[jax.ShapeDtypeStruct(shape, F32) for shape in outs],
        compiler_params=pltpu.CompilerParams(vmem_limit_bytes=limit << 20),
        cost_estimate=TINY,
        name="project",
    )(*near, *gates)


def fresh_kernel(own, sib, fresh_ref, first_ref, second_ref):
    me = lax.axis_index("ctx")
    fresh = own[...] + sib[...]
    low, high = fresh[:, :HD], fresh[:, HD:]
    fresh_ref[...] = fresh.astype(BF16)
    first_ref[...] = jnp.where(me == 0, high, low).astype(BF16)
    second_ref[...] = jnp.where(me == 3, low, high).astype(BF16)


def make_fresh(own, sib):
    rows = own.shape[0]
    out = lambda cols: jax.ShapeDtypeStruct((rows, cols), BF16)
    return pl.pallas_call(
        fresh_kernel,
        out_shape=(out(2 * HD), out(HD), out(HD)),
        compiler_params=pltpu.CompilerParams(vmem_limit_bytes=4 << 20),
        cost_estimate=TINY,
        name="fresh",
    )(own, sib)


def turn(values, cosine, sine):
    return values * cosine + pltpu.roll(values, HD // 2, 1) * sine


def assemble_kernel(fresh_ref, first_ref, second_ref, cached_ref, cos_ref, sin_ref, target_ref, key_ref, value_ref):
    me = lax.axis_index("ctx")
    low, high = fresh_ref[:, :HD].astype(F32), fresh_ref[:, HD:].astype(F32)
    first, second = first_ref[...].astype(F32), second_ref[...].astype(F32)
    fresh_key = jnp.where(me == 0, low, jnp.where(me == 3, second, first))
    fresh_value = jnp.where(me == 0, first, jnp.where(me == 3, high, second)).astype(BF16)
    fresh_key = turn(fresh_key, cos_ref[...], sin_ref[...]).astype(BF16)
    context = cached_ref.shape[0]
    count = fresh_key.shape[0]
    hit = lax.broadcasted_iota(jnp.int32, (context, count), 0) == target_ref[...]
    pick = jnp.where(hit, 1.0, 0.0)
    taken = jnp.max(pick, axis=1, keepdims=True) > 0.5
    pick = pick.astype(BF16)
    key_new = jnp.dot(pick, fresh_key, preferred_element_type=F32).astype(BF16)
    value_new = jnp.dot(pick, fresh_value, preferred_element_type=F32).astype(BF16)
    key_ref[...] = jnp.where(taken, key_new, cached_ref[:, :HD])
    value_ref[...] = jnp.where(taken, value_new, cached_ref[:, HD:]).T


def assemble(fresh, first, second, cached, cosine, sine, targets):
    context = cached.shape[0]
    return pl.pallas_call(
        assemble_kernel,
        out_shape=(
            jax.ShapeDtypeStruct((context, HD), BF16),
            jax.ShapeDtypeStruct((HD, context), BF16),
        ),
        compiler_params=pltpu.CompilerParams(vmem_limit_bytes=16 << 20),
        cost_estimate=TINY,
        name="assemble",
    )(fresh, first, second, cached, cosine, sine, targets)


def attend_kernel(heads, *refs):
    own_ref, sib_ref, key_ref, value_ref, cos_ref, sin_ref, pos_ref, key_pos_ref, *rest = refs
    out_ref = rest[-1]
    visible = key_pos_ref[...] <= pos_ref[...]
    for h in range(heads):
        cols = slice(h * HD, (h + 1) * HD)
        raw = own_ref[:, cols] + sib_ref[:, cols]
        query = (turn(raw, cos_ref[...], sin_ref[...]) * HD ** (-0.5)).astype(BF16)
        scores = lax.dot_general(
            key_ref[...], query, (((1,), (1,)), ((), ())), preferred_element_type=F32
        )
        scores = jnp.where(visible, scores, -1e30)
        exponent = jnp.exp(scores - jnp.max(scores, axis=0, keepdims=True))
        weights = exponent * (1.0 / jnp.sum(exponent, axis=0, keepdims=True))
        turned = jnp.dot(value_ref[...], weights.astype(BF16), preferred_element_type=F32)
        out_ref[:, cols] = turned.T.astype(BF16)


def attend(own, sib, shared, width, start, before):
    rec_count, cols = own.shape
    args = [own, sib, *shared]
    specs = [pl.BlockSpec(a.shape, lambda i: (0, 0)) for a in args]
    aliases = {}
    if before is not None:
        aliases = {len(args): 0}
        args.append(before)
        specs.append(pl.BlockSpec(memory_space=pltpu.HBM))
    return pl.pallas_call(
        functools.partial(attend_kernel, cols // HD),
        grid=(1,),
        in_specs=specs,
        out_specs=pl.BlockSpec((rec_count, cols), lambda i: (0, start // cols)),
        out_shape=jax.ShapeDtypeStruct((rec_count, width), BF16),
        input_output_aliases=aliases,
        compiler_params=pltpu.CompilerParams(vmem_limit_bytes=16 << 20),
        cost_estimate=TINY,
        name="attend",
    )(*args)


def fast_body(store_kv, block_slot, block_owner, rec_pos, states, w_query, w_keyval):
    store_count = lax.axis_size("store")
    ctx_count = lax.axis_size("ctx")
    my_index = lax.axis_index("ctx")
    piece_rows = store_kv.shape[1]
    block_count = block_slot.shape[1]
    rec_count = rec_pos.shape[1]
    query_cols = w_query.shape[1]
    depth = w_query.shape[0]
    positions = rec_pos[0]
    xf, yf, cf = (flip(b, store_count) for b in (XBIT, YBIT, CORE))
    by_x = lambda a: lax.ppermute(a, "store", xf)
    by_y = lambda a: lax.ppermute(a, "store", yf)
    by_core = lambda a: lax.ppermute(a, "store", cf)

    along = lambda a, pairs: lax.ppermute(a, "ctx", pairs)
    kv_cols = w_keyval.shape[1]
    late = query_cols // 2
    early = query_cols - late
    first_cols = kv_cols + early
    half = depth // 2

    asked, places = swap_ids(block_slot[0], block_owner[0], store_count)
    (w_first,) = cut(
        (w_keyval, w_query),
        [[(0, (0, 0), (0, 0), (depth, kv_cols)), (1, (0, 0), (0, kv_cols), (depth, early))]],
        [(depth, first_cols)],
    )
    first_x, first_y = by_x(w_first), by_y(w_first)
    gathered = gather_blocks(asked, store_kv, asked)
    arrived = lax.all_to_all(gathered, "store", split_axis=0, concat_axis=0, tiled=True)
    (w_last,) = cut(
        (w_query,), [[(0, (0, early), (0, 0), (depth, late))]], [(depth, late)], (arrived, first_x, first_y), limit=8
    )
    last_x, last_y = by_x(w_last), by_y(w_last)
    by_head = sort_blocks(arrived, places, (w_last,))
    cached = lax.all_to_all(by_head, "ctx", split_axis=0, concat_axis=0, tiled=True)
    cached = cached.reshape(-1, 2 * HD)

    keep, send = norm_split(states[0])
    shard, width = keep.shape
    (both,) = cut(
        (keep, by_core(send)),
        [[(0, (0, 0), (0, 0), (shard, width)), (1, (0, 0), (shard, 0), (shard, width))]],
        [(2 * shard, width)],
        near=True,
        limit=4,
    )
    along = lambda a, pairs: lax.ppermute(a, "ctx", pairs)
    two = along(both, [(0, 2), (1, 3), (2, 0), (3, 1)])
    one = along(both, [(0, 1), (1, 0), (2, 3), (3, 2)])
    up, down = relay(both, two, (one,))
    shard_parts = (
        both,
        one,
        two,
        along(up, [(1, 2), (2, 3)]),
        along(down, [(2, 1), (1, 0)]),
    )

    def diagonal(from_x, from_y, gates, limit):
        cols = from_x.shape[1]
        sent = cut(
            (from_y, from_x),
            [[(0, (0, 0), (0, 0), (half, cols))], [(1, (half, 0), (0, 0), (half, cols))]],
            [(half, cols)] * 2,
            gates,
            limit=limit,
        )
        return (by_x(sent[0]), by_y(sent[1])), sent[0]

    diag_first, _ = diagonal(first_x, first_y, (up, last_x, last_y, cached), 8)
    weights, loaded = load_weights(w_keyval, w_query, first_x, first_y, last_x, last_y)
    diag_last, sent_last = diagonal(last_x, last_y, (loaded,), 6)

    shard_rows = block_count * piece_rows
    frequency = jnp.exp(
        jnp.arange(HD // 2, dtype=F32) * (-2.0 * math.log(500000.0) / HD)
    )
    angles = positions.astype(F32)[:, None] * frequency[None, :]
    cos_half, sin_half = jnp.cos(angles), jnp.sin(angles)
    cosine = jnp.concatenate((cos_half, cos_half), axis=1)
    sine = jnp.concatenate((-sin_half, sin_half), axis=1)
    block_len = piece_rows * ctx_count
    targets = (
        positions % block_len // piece_rows * shard_rows
        + positions // block_len * piece_rows
        + positions % piece_rows
    )

    row_ids = jnp.arange(ctx_count * shard_rows)
    key_pos = (
        row_ids % shard_rows // piece_rows * block_len
        + row_ids // shard_rows * piece_rows
        + row_ids % piece_rows
    )

    rows = load_rows(shard_parts, sent_last)
    first_part, last_part = project(
        project_near_kernel,
        (rows, weights),
        (),
        [(2 * rec_count, first_cols), (2 * rec_count, late)],
        20,
    )
    kv_own, kv_sib, early_own, early_sib = project(
        project_first_kernel,
        (rows, *diag_first, first_part),
        (),
        [(rec_count, kv_cols)] * 2 + [(rec_count, early)] * 2,
        14,
    )
    fresh, to_first, to_second = make_fresh(kv_own, by_core(kv_sib))
    first = along(to_first, [(0, 1), (1, 2), (2, 0)])
    second = along(to_second, [(1, 3), (2, 1), (3, 2)])
    key_rows, value_rows = assemble(
        fresh, first, second, cached, cosine, sine, targets.reshape(1, rec_count)
    )
    shared = (
        key_rows,
        value_rows,
        cosine,
        sine,
        positions.reshape(1, rec_count),
        key_pos.reshape(-1, 1),
    )
    result = attend(early_own, by_core(early_sib), shared, query_cols, 0, None)
    own, sib = project(
        project_last_kernel,
        (rows, *diag_last, last_part),
        (first, second, cached),
        [(rec_count, late)] * 2,
        12,
    )
    result = attend(own, by_core(sib), shared, query_cols, early, result)
    return result.reshape(1, rec_count, query_cols)


def solution(mesh):
    fast = mesh.shape["store"] == 8 and mesh.shape["ctx"] == KVH
    return jax.shard_map(
        fast_body if fast else general_body,
        mesh=mesh,
        in_specs=(
            P("store", "ctx", None),
            P("store", None),
            P("store", None),
            P("store", None),
            P("store", "ctx", None),
            P("store", "ctx"),
            P("store", "ctx"),
        ),
        out_specs=P("store", None, "ctx"),
        check_vma=False,
    )
```

```python
import functools
import math

import jax
import jax.numpy as jnp
from jax import lax
from jax.experimental import pallas as pl
from jax.experimental.pallas import tpu as pltpu
from jax.sharding import PartitionSpec as P

QH = 32
KVH = 4
HD = 128
CAP = 2
F32 = jnp.float32
BF16 = jnp.bfloat16
TINY = pl.CostEstimate(flops=1, bytes_accessed=1, transcendentals=0)


def rotate(values, positions):
    midpoint = values.shape[-1] // 2
    frequency = jnp.exp(
        jnp.arange(midpoint, dtype=jnp.float32) * (-2.0 * math.log(500000.0) / values.shape[-1])
    )
    angles = positions.astype(jnp.float32)[:, None] * frequency[None, :]
    cosine = jnp.cos(angles)[:, None, :]
    sine_term = jnp.sin(angles)[:, None, :]
    leading = values[..., :midpoint]
    trailing = values[..., midpoint:]
    return jnp.concatenate(
        (leading * cosine - trailing * sine_term, trailing * cosine + leading * sine_term), axis=-1
    )


def normalize(states):
    floated = states.astype(jnp.float32)
    return (
        floated * lax.rsqrt(jnp.mean(floated * floated, axis=-1, keepdims=True) + 1e-05)
    ).astype(jnp.bfloat16)


def swap_ids(slot_ids, owners, store_count):
    block_count = slot_ids.shape[0]
    slot_order = jnp.arange(block_count)
    earlier = slot_order[None, :] < slot_order[:, None]
    slot_ranks = jnp.sum((owners[:, None] == owners[None, :]) & earlier, axis=1)
    slot_hits = (owners[:, None, None] == jnp.arange(store_count)[None, :, None]) & (
        slot_ranks[:, None, None] == jnp.arange(CAP)[None, None, :]
    )
    wanted = jnp.sum(jnp.where(slot_hits, slot_ids[:, None, None], 0), axis=0)
    asked = lax.all_to_all(wanted, "store", split_axis=0, concat_axis=0, tiled=True)
    return asked, owners * CAP + slot_ranks


def fetch_blocks(store_kv, asked, places):
    arrived = lax.all_to_all(store_kv[asked], "store", split_axis=0, concat_axis=0, tiled=True)
    return arrived.reshape((-1,) + store_kv.shape[1:])[places].reshape(-1, store_kv.shape[2])


def general_body(store_kv, block_slot, block_owner, rec_pos, states, w_query, w_keyval):
    ctx_count = lax.axis_size("ctx")
    my_index = lax.axis_index("ctx")
    piece_rows = store_kv.shape[1]
    block_count = block_slot.shape[1]
    rec_count = rec_pos.shape[1]
    positions = rec_pos[0]
    shard_rows = block_count * piece_rows
    local_rows = fetch_blocks(
        store_kv, *swap_ids(block_slot[0], block_owner[0], lax.axis_size("store"))
    )
    normed = normalize(states[0])
    query_cols = w_query.shape[1]
    query_weight, keyval_weight = (
        lax.all_gather(w_query, "store", axis=0, tiled=True),
        lax.all_gather(w_keyval, "store", axis=0, tiled=True),
    )
    row_piece = lax.all_gather(normed, "ctx", axis=0, tiled=True)
    query_raw = jnp.dot(row_piece, query_weight, preferred_element_type=jnp.float32)
    keyval_raw = jnp.dot(row_piece, keyval_weight, preferred_element_type=jnp.float32)
    heads_here = query_cols // HD
    group_size = QH // KVH
    queries = (
        rotate(query_raw.reshape(rec_count, heads_here, HD), positions) * HD ** (-0.5)
    ).astype(jnp.bfloat16)
    fresh_rows = lax.all_gather(keyval_raw.astype(jnp.bfloat16), "ctx", axis=1, tiled=True)
    shared_head = my_index * heads_here // group_size
    fresh_key = rotate(
        lax.dynamic_slice_in_dim(fresh_rows, shared_head * HD, HD, 1)
        .astype(jnp.float32)
        .reshape(rec_count, 1, HD),
        positions,
    )
    fresh_key = fresh_key.astype(jnp.bfloat16).reshape(rec_count, HD)
    fresh_value = lax.dynamic_slice_in_dim(fresh_rows, KVH * HD + shared_head * HD, HD, 1)
    gathered = lax.all_gather(local_rows, "ctx", axis=0, tiled=True)
    key_rows = lax.dynamic_slice_in_dim(gathered, shared_head * HD, HD, 1)
    value_rows = lax.dynamic_slice_in_dim(gathered, KVH * HD + shared_head * HD, HD, 1)
    row_ids = jnp.arange(ctx_count * shard_rows)
    block_len = piece_rows * ctx_count
    key_pos = (
        row_ids % shard_rows // piece_rows * block_len
        + row_ids // shard_rows * piece_rows
        + row_ids % piece_rows
    )
    targets = (
        positions % block_len // piece_rows * shard_rows
        + positions // block_len * piece_rows
        + positions % piece_rows
    )
    key_rows = key_rows.at[targets].set(fresh_key)
    value_rows = value_rows.at[targets].set(fresh_value)
    scores = jnp.einsum("rhd,cd->hrc", queries, key_rows, preferred_element_type=jnp.float32)
    visible = key_pos[None, None, :] <= positions[None, :, None]
    scores = jnp.where(visible, scores, -1e30)
    row_max = jnp.max(scores, axis=-1, keepdims=True)
    exponent = jnp.exp(scores - row_max)
    weights = (exponent / jnp.sum(exponent, axis=-1, keepdims=True)).astype(jnp.bfloat16)
    attended = jnp.einsum("hrc,cd->rhd", weights, value_rows, preferred_element_type=jnp.float32)
    return attended.reshape(1, rec_count, heads_here * HD).astype(jnp.bfloat16)


CORE, XBIT, YBIT = 1, 2, 4


def flip(bit, count):
    return [(s, s ^ bit) for s in range(count)]


def norm_kernel(states_ref, keep_ref, send_ref):
    me = lax.axis_index("store")
    width = states_ref.shape[1]
    depth = width // 8
    total = jnp.zeros((states_ref.shape[0], 1), F32)
    for s in range(8):
        part = states_ref[:, s * depth : (s + 1) * depth].astype(F32)
        total += jnp.sum(part * part, axis=1, keepdims=True)
    scale = lax.rsqrt(total / width + 1e-05)
    for r in range(4):
        for core, out in ((0, keep_ref), (1, send_ref)):
            s = lax.bitwise_xor(me, r * 2 + core)
            part = states_ref[:, pl.ds(pl.multiple_of(s * depth, depth), depth)].astype(F32)
            out[:, r * depth : (r + 1) * depth] = (part * scale).astype(BF16)


def norm_split(states):
    rows, width = states.shape
    half = jax.ShapeDtypeStruct((rows, width // 2), BF16)
    return pl.pallas_call(
        norm_kernel,
        out_shape=(half, half),
        compiler_params=pltpu.CompilerParams(vmem_limit_bytes=16 << 20),
        cost_estimate=TINY,
        name="norm_split",
    )(states)


def cut_kernel(plan, n_in, *refs):
    outs, sems = refs[n_in:-1], refs[-1]
    copies = []
    for out, pieces in zip(outs, plan):
        for source, (row, col), (to_row, to_col), (rows, cols) in pieces:
            copies.append(
                pltpu.make_async_copy(
                    refs[source].at[pl.ds(row, rows), pl.ds(col, cols)],
                    out.at[pl.ds(to_row, rows), pl.ds(to_col, cols)],
                    sems.at[len(copies)],
                )
            )
    for copy in copies:
        copy.start()
    for copy in copies:
        copy.wait()


def cut(sources, plan, shapes, gates=(), near=False, limit=58):
    gates = jax.tree.leaves(gates)
    args = [*sources, *gates]
    hbm = pl.BlockSpec(memory_space=pltpu.HBM)
    vmem = pl.BlockSpec(memory_space=pltpu.VMEM)
    anywhere = pl.BlockSpec(memory_space=pl.ANY)
    return pl.pallas_call(
        functools.partial(cut_kernel, plan, len(args)),
        in_specs=[vmem if near else hbm] * len(sources) + [anywhere] * len(gates),
        out_specs=[hbm if near else vmem] * len(shapes),
        out_shape=[jax.ShapeDtypeStruct(shape, BF16) for shape in shapes],
        scratch_shapes=[pltpu.SemaphoreType.DMA((sum(len(p) for p in plan),))],
        compiler_params=pltpu.CompilerParams(vmem_limit_bytes=limit << 20),
        cost_estimate=TINY,
        name="cut",
    )(*args)


def relay_kernel(own, two, *refs):
    up, down, sems = refs[-3:]
    me = lax.axis_index("ctx")

    def moves(act):
        for way, out in enumerate((up, down)):
            for source, chosen in ((own, me == 1 + way), (two, me != 1 + way)):

                @pl.when(chosen)
                def _():
                    act(pltpu.make_async_copy(source, out, sems.at[way]))

    moves(lambda c: c.start())
    moves(lambda c: c.wait())


def relay(own, two, gates):
    hbm = pl.BlockSpec(memory_space=pltpu.HBM)
    out = jax.ShapeDtypeStruct(own.shape, BF16)
    return pl.pallas_call(
        relay_kernel,
        in_specs=[hbm] * 2 + [pl.BlockSpec(memory_space=pl.ANY)] * len(gates),
        out_shape=(out, out),
        scratch_shapes=[pltpu.SemaphoreType.DMA((2,))],
        compiler_params=pltpu.CompilerParams(vmem_limit_bytes=4 << 20),
        cost_estimate=TINY,
        name="relay",
    )(own, two, *gates)


def sort_kernel(blocks_ref, places_ref, *refs):
    out_ref = refs[-1]
    heads = out_ref.shape[0]
    size = blocks_ref.shape[1]
    for j in range(places_ref.shape[0]):
        block = blocks_ref[places_ref[j]]
        for h in range(heads):
            rows = slice(j * size, (j + 1) * size)
            out_ref[h, rows, :HD] = block[:, h * HD : (h + 1) * HD]
            out_ref[h, rows, HD:] = block[:, (heads + h) * HD : (heads + h + 1) * HD]


def sort_blocks(blocks, places, gates):
    anywhere = pl.BlockSpec(memory_space=pl.ANY)
    count, size, _ = blocks.shape
    return pl.pallas_call(
        sort_kernel,
        in_specs=[pl.BlockSpec(memory_space=pltpu.VMEM), pl.BlockSpec(memory_space=pltpu.SMEM)]
        + [anywhere] * len(gates),
        out_shape=jax.ShapeDtypeStruct((KVH, places.shape[0] * size, 2 * HD), BF16),
        compiler_params=pltpu.CompilerParams(vmem_limit_bytes=4 << 20),
        cost_estimate=TINY,
        name="sort_blocks",
    )(blocks, places, *gates)


STEP = 2 * HD


def share(total, shards, own, sib, cols):
    rows = own.shape[0] // shards
    for z in range(shards):
        here = slice(z * rows, (z + 1) * rows)
        own[here, cols] = total[2 * z * rows : (2 * z + 1) * rows]
        sib[here, cols] = total[(2 * z + 1) * rows : (2 * z + 2) * rows]


def hold_kernel(*refs):
    pass


def hold(first, second, gates):
    anywhere = pl.BlockSpec(memory_space=pl.ANY)
    return pl.pallas_call(
        hold_kernel,
        in_specs=[anywhere] * (2 + len(gates)),
        out_specs=[anywhere] * 2,
        out_shape=[jax.ShapeDtypeStruct(first.shape, BF16)] * 2,
        input_output_aliases={0: 0, 1: 1},
        compiler_params=pltpu.CompilerParams(vmem_limit_bytes=2 << 20),
        cost_estimate=TINY,
        name="hold",
    )(first, second, *gates)


def load_rows_kernel(*refs):
    parts, out_ref, sems = refs[:5], refs[-2], refs[-1]
    me = lax.axis_index("ctx")
    rows = parts[0].shape[0]

    def copies(act):
        for k in range(4):
            start = pl.multiple_of(lax.bitwise_xor(me, k) * rows, rows)
            target = out_ref.at[pl.ds(start, rows)]
            if k < 3:
                act(pltpu.make_async_copy(parts[k], target, sems.at[k]))
            else:
                for source, chosen in ((parts[3], me >= 2), (parts[4], me < 2)):

                    @pl.when(chosen)
                    def _():
                        act(pltpu.make_async_copy(source, target, sems.at[k]))

    copies(lambda c: c.start())
    copies(lambda c: c.wait())


def load_rows(parts, gate):
    rows, width = parts[0].shape
    return pl.pallas_call(
        load_rows_kernel,
        in_specs=[pl.BlockSpec(memory_space=pltpu.HBM)] * 5 + [pl.BlockSpec(memory_space=pl.ANY)],
        out_shape=jax.ShapeDtypeStruct((4 * rows, width), BF16),
        scratch_shapes=[pltpu.SemaphoreType.DMA((4,))],
        compiler_params=pltpu.CompilerParams(vmem_limit_bytes=12 << 20),
        cost_estimate=TINY,
        name="load_rows",
    )(*parts, gate)


def load_weights_kernel(kv, q, first_x, first_y, last_x, last_y, out_ref, token, sems):
    depth = kv.shape[0]
    copies = []
    for r, sources in enumerate(((kv, q), (first_x, last_x), (first_y, last_y))):
        col = 0
        for source in sources:
            width = source.shape[1]
            target = out_ref.at[pl.ds(r * depth, depth), pl.ds(col, width)]
            copies.append(pltpu.make_async_copy(source, target, sems.at[len(copies)]))
            col += width
    for copy in copies:
        copy.start()
    token[...] = jnp.zeros(token.shape, F32)
    for copy in copies:
        copy.wait()


def load_weights(*parts):
    depth = parts[0].shape[0]
    cols = parts[0].shape[1] + parts[1].shape[1]
    return pl.pallas_call(
        load_weights_kernel,
        in_specs=[pl.BlockSpec(memory_space=pltpu.HBM)] * 6,
        out_shape=(
            jax.ShapeDtypeStruct((3 * depth, cols), BF16),
            jax.ShapeDtypeStruct((8, HD), F32),
        ),
        scratch_shapes=[pltpu.SemaphoreType.DMA((6,))],
        compiler_params=pltpu.CompilerParams(vmem_limit_bytes=16 << 20),
        cost_estimate=TINY,
        name="load_weights",
    )(*parts)


def gather_kernel(asked_ref, store_ref, *refs):
    out_ref, sems = refs[-2:]
    owners, cap = asked_ref.shape
    copies = [
        pltpu.make_async_copy(
            store_ref.at[asked_ref[i, j]], out_ref.at[i * cap + j], sems.at[i * cap + j]
        )
        for i in range(owners)
        for j in range(cap)
    ]
    for copy in copies:
        copy.start()
    for copy in copies:
        copy.wait()


def gather_blocks(asked, store_kv, gate):
    return pl.pallas_call(
        gather_kernel,
        in_specs=[
            pl.BlockSpec(memory_space=pltpu.SMEM),
            pl.BlockSpec(memory_space=pltpu.HBM),
            pl.BlockSpec(memory_space=pl.ANY),
        ],
        out_shape=jax.ShapeDtypeStruct((asked.size,) + store_kv.shape[1:], BF16),
        scratch_shapes=[pltpu.SemaphoreType.DMA((asked.size,))],
        compiler_params=pltpu.CompilerParams(vmem_limit_bytes=4 << 20),
        cost_estimate=TINY,
        name="gather_blocks",
    )(asked, store_kv, gate)


def diagonal_part(a_ref, d_x, d_y, col):
    h = d_x.shape[0]
    part = jnp.dot(a_ref[:, 6 * h : 7 * h], d_x[:, col : col + STEP], preferred_element_type=F32)
    return part + jnp.dot(a_ref[:, 7 * h :], d_y[:, col : col + STEP], preferred_element_type=F32)


def project_near_kernel(a_ref, w_ref, first, last):
    depth = w_ref.shape[0] // 3
    col = 0
    for out in (first, last):
        for here in range(0, out.shape[1], STEP):
            total = 0.0
            for r in range(3):
                part = slice(r * depth, (r + 1) * depth)
                total += jnp.dot(
                    a_ref[:, part], w_ref[part, col : col + STEP], preferred_element_type=F32
                )
            out[:, here : here + STEP] = total
            col += STEP


def project_first_kernel(a_ref, d_x, d_y, rest, kv_own, kv_sib, own, sib):
    for col in range(0, rest.shape[1], STEP):
        total = rest[:, col : col + STEP] + diagonal_part(a_ref, d_x, d_y, col)
        if col == 0:
            share(total, 4, kv_own, kv_sib, slice(0, STEP))
        else:
            share(total, 4, own, sib, slice(col - STEP, col))


def project_last_kernel(a_ref, d_x, d_y, rest, *refs):
    own, sib = refs[-2:]
    for col in range(0, rest.shape[1], STEP):
        total = rest[:, col : col + STEP] + diagonal_part(a_ref, d_x, d_y, col)
        share(total, 4, own, sib, slice(col, col + STEP))


def project(kernel, near, gates, outs, limit):
    vmem = pl.BlockSpec(memory_space=pltpu.VMEM)
    return pl.pallas_call(
        kernel,
        in_specs=[vmem] * len(near) + [pl.BlockSpec(memory_space=pl.ANY)] * len(gates),
        out_shape=[jax.ShapeDtypeStruct(shape, F32) for shape in outs],
        compiler_params=pltpu.CompilerParams(vmem_limit_bytes=limit << 20),
        cost_estimate=TINY,
        name="project",
    )(*near, *gates)


def fresh_kernel(own, sib, fresh_ref, first_ref, second_ref):
    me = lax.axis_index("ctx")
    fresh = own[...] + sib[...]
    low, high = fresh[:, :HD], fresh[:, HD:]
    fresh_ref[...] = fresh.astype(BF16)
    first_ref[...] = jnp.where(me == 0, high, low).astype(BF16)
    second_ref[...] = jnp.where(me == 3, low, high).astype(BF16)


def make_fresh(own, sib):
    rows = own.shape[0]
    out = lambda cols: jax.ShapeDtypeStruct((rows, cols), BF16)
    return pl.pallas_call(
        fresh_kernel,
        out_shape=(out(2 * HD), out(HD), out(HD)),
        compiler_params=pltpu.CompilerParams(vmem_limit_bytes=4 << 20),
        cost_estimate=TINY,
        name="fresh",
    )(own, sib)


def turn(values, cosine, sine):
    return values * cosine + pltpu.roll(values, HD // 2, 1) * sine


def assemble_kernel(fresh_ref, first_ref, second_ref, cached_ref, cos_ref, sin_ref, target_ref, key_ref, value_ref):
    me = lax.axis_index("ctx")
    low, high = fresh_ref[:, :HD].astype(F32), fresh_ref[:, HD:].astype(F32)
    first, second = first_ref[...].astype(F32), second_ref[...].astype(F32)
    fresh_key = jnp.where(me == 0, low, jnp.where(me == 3, second, first))
    fresh_value = jnp.where(me == 0, first, jnp.where(me == 3, high, second)).astype(BF16)
    fresh_key = turn(fresh_key, cos_ref[...], sin_ref[...]).astype(BF16)
    context = cached_ref.shape[0]
    count = fresh_key.shape[0]
    hit = lax.broadcasted_iota(jnp.int32, (context, count), 0) == target_ref[...]
    pick = jnp.where(hit, 1.0, 0.0)
    taken = jnp.max(pick, axis=1, keepdims=True) > 0.5
    pick = pick.astype(BF16)
    key_new = jnp.dot(pick, fresh_key, preferred_element_type=F32).astype(BF16)
    value_new = jnp.dot(pick, fresh_value, preferred_element_type=F32).astype(BF16)
    key_ref[...] = jnp.where(taken, key_new, cached_ref[:, :HD])
    value_ref[...] = jnp.where(taken, value_new, cached_ref[:, HD:]).T


def assemble(fresh, first, second, cached, cosine, sine, targets):
    context = cached.shape[0]
    return pl.pallas_call(
        assemble_kernel,
        out_shape=(
            jax.ShapeDtypeStruct((context, HD), BF16),
            jax.ShapeDtypeStruct((HD, context), BF16),
        ),
        compiler_params=pltpu.CompilerParams(vmem_limit_bytes=16 << 20),
        cost_estimate=TINY,
        name="assemble",
    )(fresh, first, second, cached, cosine, sine, targets)


def attend_kernel(heads, *refs):
    own_ref, sib_ref, key_ref, value_ref, cos_ref, sin_ref, pos_ref, key_pos_ref, *rest = refs
    out_ref = rest[-1]
    visible = key_pos_ref[...] <= pos_ref[...]
    for h in range(heads):
        cols = slice(h * HD, (h + 1) * HD)
        raw = own_ref[:, cols] + sib_ref[:, cols]
        query = (turn(raw, cos_ref[...], sin_ref[...]) * HD ** (-0.5)).astype(BF16)
        scores = lax.dot_general(
            key_ref[...], query, (((1,), (1,)), ((), ())), preferred_element_type=F32
        )
        scores = jnp.where(visible, scores, -1e30)
        exponent = jnp.exp(scores - jnp.max(scores, axis=0, keepdims=True))
        weights = exponent * (1.0 / jnp.sum(exponent, axis=0, keepdims=True))
        turned = jnp.dot(value_ref[...], weights.astype(BF16), preferred_element_type=F32)
        out_ref[:, cols] = turned.T.astype(BF16)


def attend(own, sib, shared, width, start, before):
    rec_count, cols = own.shape
    args = [own, sib, *shared]
    specs = [pl.BlockSpec(a.shape, lambda i: (0, 0)) for a in args]
    aliases = {}
    if before is not None:
        aliases = {len(args): 0}
        args.append(before)
        specs.append(pl.BlockSpec(memory_space=pltpu.HBM))
    return pl.pallas_call(
        functools.partial(attend_kernel, cols // HD),
        grid=(1,),
        in_specs=specs,
        out_specs=pl.BlockSpec((rec_count, cols), lambda i: (0, start // cols)),
        out_shape=jax.ShapeDtypeStruct((rec_count, width), BF16),
        input_output_aliases=aliases,
        compiler_params=pltpu.CompilerParams(vmem_limit_bytes=16 << 20),
        cost_estimate=TINY,
        name="attend",
    )(*args)


def fast_body(store_kv, block_slot, block_owner, rec_pos, states, w_query, w_keyval):
    store_count = lax.axis_size("store")
    ctx_count = lax.axis_size("ctx")
    my_index = lax.axis_index("ctx")
    piece_rows = store_kv.shape[1]
    block_count = block_slot.shape[1]
    rec_count = rec_pos.shape[1]
    query_cols = w_query.shape[1]
    depth = w_query.shape[0]
    positions = rec_pos[0]
    xf, yf, cf = (flip(b, store_count) for b in (XBIT, YBIT, CORE))
    by_x = lambda a: lax.ppermute(a, "store", xf)
    by_y = lambda a: lax.ppermute(a, "store", yf)
    by_core = lambda a: lax.ppermute(a, "store", cf)

    along = lambda a, pairs: lax.ppermute(a, "ctx", pairs)
    kv_cols = w_keyval.shape[1]
    late = query_cols // 2
    early = query_cols - late
    first_cols = kv_cols + early
    half = depth // 2

    asked, places = swap_ids(block_slot[0], block_owner[0], store_count)
    (w_first,) = cut(
        (w_keyval, w_query),
        [[(0, (0, 0), (0, 0), (depth, kv_cols)), (1, (0, 0), (0, kv_cols), (depth, early))]],
        [(depth, first_cols)],
    )
    first_x, first_y = by_x(w_first), by_y(w_first)
    gathered = gather_blocks(asked, store_kv, asked)
    arrived = lax.all_to_all(gathered, "store", split_axis=0, concat_axis=0, tiled=True)
    (w_last,) = cut(
        (w_query,), [[(0, (0, early), (0, 0), (depth, late))]], [(depth, late)], (arrived, first_x, first_y), limit=8
    )
    last_x, last_y = by_x(w_last), by_y(w_last)
    by_head = sort_blocks(arrived, places, (w_last,))
    cached = lax.all_to_all(by_head, "ctx", split_axis=0, concat_axis=0, tiled=True)
    cached = cached.reshape(-1, 2 * HD)

    keep, send = norm_split(states[0])
    shard, width = keep.shape
    (both,) = cut(
        (keep, by_core(send)),
        [[(0, (0, 0), (0, 0), (shard, width)), (1, (0, 0), (shard, 0), (shard, width))]],
        [(2 * shard, width)],
        near=True,
        limit=4,
    )
    along = lambda a, pairs: lax.ppermute(a, "ctx", pairs)
    two = along(both, [(0, 2), (1, 3), (2, 0), (3, 1)])
    one = along(both, [(0, 1), (1, 0), (2, 3), (3, 2)])
    up, down = relay(both, two, (one,))
    shard_parts = (
        both,
        one,
        two,
        along(up, [(1, 2), (2, 3)]),
        along(down, [(2, 1), (1, 0)]),
    )

    def diagonal(from_x, from_y, gates, limit, late_gates=()):
        cols = from_x.shape[1]
        sent = cut(
            (from_y, from_x),
            [[(0, (0, 0), (0, 0), (half, cols))], [(1, (half, 0), (0, 0), (half, cols))]],
            [(half, cols)] * 2,
            gates,
            limit=limit,
        )
        if late_gates:
            sent = hold(*sent, late_gates)
        return (by_x(sent[0]), by_y(sent[1])), sent[0]

    diag_first, _ = diagonal(first_x, first_y, (up, cached), 8, (last_x, last_y))
    weights, loaded = load_weights(w_keyval, w_query, first_x, first_y, last_x, last_y)
    diag_last, sent_last = diagonal(last_x, last_y, (loaded,), 6)

    shard_rows = block_count * piece_rows
    frequency = jnp.exp(
        jnp.arange(HD // 2, dtype=F32) * (-2.0 * math.log(500000.0) / HD)
    )
    angles = positions.astype(F32)[:, None] * frequency[None, :]
    cos_half, sin_half = jnp.cos(angles), jnp.sin(angles)
    cosine = jnp.concatenate((cos_half, cos_half), axis=1)
    sine = jnp.concatenate((-sin_half, sin_half), axis=1)
    block_len = piece_rows * ctx_count
    targets = (
        positions % block_len // piece_rows * shard_rows
        + positions // block_len * piece_rows
        + positions % piece_rows
    )

    row_ids = jnp.arange(ctx_count * shard_rows)
    key_pos = (
        row_ids % shard_rows // piece_rows * block_len
        + row_ids // shard_rows * piece_rows
        + row_ids % piece_rows
    )

    rows = load_rows(shard_parts, sent_last)
    first_part, last_part = project(
        project_near_kernel,
        (rows, weights),
        (),
        [(2 * rec_count, first_cols), (2 * rec_count, late)],
        20,
    )
    kv_own, kv_sib, early_own, early_sib = project(
        project_first_kernel,
        (rows, *diag_first, first_part),
        (),
        [(rec_count, kv_cols)] * 2 + [(rec_count, early)] * 2,
        14,
    )
    fresh, to_first, to_second = make_fresh(kv_own, by_core(kv_sib))
    first = along(to_first, [(0, 1), (1, 2), (2, 0)])
    second = along(to_second, [(1, 3), (2, 1), (3, 2)])
    key_rows, value_rows = assemble(
        fresh, first, second, cached, cosine, sine, targets.reshape(1, rec_count)
    )
    shared = (
        key_rows,
        value_rows,
        cosine,
        sine,
        positions.reshape(1, rec_count),
        key_pos.reshape(-1, 1),
    )
    result = attend(early_own, by_core(early_sib), shared, query_cols, 0, None)
    own, sib = project(
        project_last_kernel,
        (rows, *diag_last, last_part),
        (first, second, cached),
        [(rec_count, late)] * 2,
        12,
    )
    result = attend(own, by_core(sib), shared, query_cols, early, result)
    return result.reshape(1, rec_count, query_cols)


def solution(mesh):
    fast = mesh.shape["store"] == 8 and mesh.shape["ctx"] == KVH
    return jax.shard_map(
        fast_body if fast else general_body,
        mesh=mesh,
        in_specs=(
            P("store", "ctx", None),
            P("store", None),
            P("store", None),
            P("store", None),
            P("store", "ctx", None),
            P("store", "ctx"),
            P("store", "ctx"),
        ),
        out_specs=P("store", None, "ctx"),
        check_vma=False,
    )
```

```python
import functools
import math

import jax
import jax.numpy as jnp
from jax import lax
from jax.experimental import pallas as pl
from jax.experimental.pallas import tpu as pltpu
from jax.sharding import PartitionSpec as P

QH = 32
KVH = 4
HD = 128
CAP = 2
F32 = jnp.float32
BF16 = jnp.bfloat16
TINY = pl.CostEstimate(flops=1, bytes_accessed=1, transcendentals=0)


def rotate(values, positions):
    midpoint = values.shape[-1] // 2
    frequency = jnp.exp(
        jnp.arange(midpoint, dtype=jnp.float32) * (-2.0 * math.log(500000.0) / values.shape[-1])
    )
    angles = positions.astype(jnp.float32)[:, None] * frequency[None, :]
    cosine = jnp.cos(angles)[:, None, :]
    sine_term = jnp.sin(angles)[:, None, :]
    leading = values[..., :midpoint]
    trailing = values[..., midpoint:]
    return jnp.concatenate(
        (leading * cosine - trailing * sine_term, trailing * cosine + leading * sine_term), axis=-1
    )


def normalize(states):
    floated = states.astype(jnp.float32)
    return (
        floated * lax.rsqrt(jnp.mean(floated * floated, axis=-1, keepdims=True) + 1e-05)
    ).astype(jnp.bfloat16)


def swap_ids(slot_ids, owners, store_count):
    block_count = slot_ids.shape[0]
    slot_order = jnp.arange(block_count)
    earlier = slot_order[None, :] < slot_order[:, None]
    slot_ranks = jnp.sum((owners[:, None] == owners[None, :]) & earlier, axis=1)
    slot_hits = (owners[:, None, None] == jnp.arange(store_count)[None, :, None]) & (
        slot_ranks[:, None, None] == jnp.arange(CAP)[None, None, :]
    )
    wanted = jnp.sum(jnp.where(slot_hits, slot_ids[:, None, None], 0), axis=0)
    asked = lax.all_to_all(wanted, "store", split_axis=0, concat_axis=0, tiled=True)
    return asked, owners * CAP + slot_ranks


def fetch_blocks(store_kv, asked, places):
    arrived = lax.all_to_all(store_kv[asked], "store", split_axis=0, concat_axis=0, tiled=True)
    return arrived.reshape((-1,) + store_kv.shape[1:])[places].reshape(-1, store_kv.shape[2])


def general_body(store_kv, block_slot, block_owner, rec_pos, states, w_query, w_keyval):
    ctx_count = lax.axis_size("ctx")
    my_index = lax.axis_index("ctx")
    piece_rows = store_kv.shape[1]
    block_count = block_slot.shape[1]
    rec_count = rec_pos.shape[1]
    positions = rec_pos[0]
    shard_rows = block_count * piece_rows
    local_rows = fetch_blocks(
        store_kv, *swap_ids(block_slot[0], block_owner[0], lax.axis_size("store"))
    )
    normed = normalize(states[0])
    query_cols = w_query.shape[1]
    query_weight, keyval_weight = (
        lax.all_gather(w_query, "store", axis=0, tiled=True),
        lax.all_gather(w_keyval, "store", axis=0, tiled=True),
    )
    row_piece = lax.all_gather(normed, "ctx", axis=0, tiled=True)
    query_raw = jnp.dot(row_piece, query_weight, preferred_element_type=jnp.float32)
    keyval_raw = jnp.dot(row_piece, keyval_weight, preferred_element_type=jnp.float32)
    heads_here = query_cols // HD
    group_size = QH // KVH
    queries = (
        rotate(query_raw.reshape(rec_count, heads_here, HD), positions) * HD ** (-0.5)
    ).astype(jnp.bfloat16)
    fresh_rows = lax.all_gather(keyval_raw.astype(jnp.bfloat16), "ctx", axis=1, tiled=True)
    shared_head = my_index * heads_here // group_size
    fresh_key = rotate(
        lax.dynamic_slice_in_dim(fresh_rows, shared_head * HD, HD, 1)
        .astype(jnp.float32)
        .reshape(rec_count, 1, HD),
        positions,
    )
    fresh_key = fresh_key.astype(jnp.bfloat16).reshape(rec_count, HD)
    fresh_value = lax.dynamic_slice_in_dim(fresh_rows, KVH * HD + shared_head * HD, HD, 1)
    gathered = lax.all_gather(local_rows, "ctx", axis=0, tiled=True)
    key_rows = lax.dynamic_slice_in_dim(gathered, shared_head * HD, HD, 1)
    value_rows = lax.dynamic_slice_in_dim(gathered, KVH * HD + shared_head * HD, HD, 1)
    row_ids = jnp.arange(ctx_count * shard_rows)
    block_len = piece_rows * ctx_count
    key_pos = (
        row_ids % shard_rows // piece_rows * block_len
        + row_ids // shard_rows * piece_rows
        + row_ids % piece_rows
    )
    targets = (
        positions % block_len // piece_rows * shard_rows
        + positions // block_len * piece_rows
        + positions % piece_rows
    )
    key_rows = key_rows.at[targets].set(fresh_key)
    value_rows = value_rows.at[targets].set(fresh_value)
    scores = jnp.einsum("rhd,cd->hrc", queries, key_rows, preferred_element_type=jnp.float32)
    visible = key_pos[None, None, :] <= positions[None, :, None]
    scores = jnp.where(visible, scores, -1e30)
    row_max = jnp.max(scores, axis=-1, keepdims=True)
    exponent = jnp.exp(scores - row_max)
    weights = (exponent / jnp.sum(exponent, axis=-1, keepdims=True)).astype(jnp.bfloat16)
    attended = jnp.einsum("hrc,cd->rhd", weights, value_rows, preferred_element_type=jnp.float32)
    return attended.reshape(1, rec_count, heads_here * HD).astype(jnp.bfloat16)


CORE, XBIT, YBIT = 1, 2, 4


def flip(bit, count):
    return [(s, s ^ bit) for s in range(count)]


def norm_kernel(states_ref, keep_ref, send_ref):
    me = lax.axis_index("store")
    width = states_ref.shape[1]
    depth = width // 8
    total = jnp.zeros((states_ref.shape[0], 1), F32)
    for s in range(8):
        part = states_ref[:, s * depth : (s + 1) * depth].astype(F32)
        total += jnp.sum(part * part, axis=1, keepdims=True)
    scale = lax.rsqrt(total / width + 1e-05)
    for r in range(4):
        for core, out in ((0, keep_ref), (1, send_ref)):
            s = lax.bitwise_xor(me, r * 2 + core)
            part = states_ref[:, pl.ds(pl.multiple_of(s * depth, depth), depth)].astype(F32)
            out[:, r * depth : (r + 1) * depth] = (part * scale).astype(BF16)


def norm_split(states):
    rows, width = states.shape
    half = jax.ShapeDtypeStruct((rows, width // 2), BF16)
    return pl.pallas_call(
        norm_kernel,
        out_shape=(half, half),
        compiler_params=pltpu.CompilerParams(vmem_limit_bytes=16 << 20),
        cost_estimate=TINY,
        name="norm_split",
    )(states)


def cut_kernel(plan, n_in, *refs):
    outs, sems = refs[n_in:-1], refs[-1]
    copies = []
    for out, pieces in zip(outs, plan):
        for source, (row, col), (to_row, to_col), (rows, cols) in pieces:
            copies.append(
                pltpu.make_async_copy(
                    refs[source].at[pl.ds(row, rows), pl.ds(col, cols)],
                    out.at[pl.ds(to_row, rows), pl.ds(to_col, cols)],
                    sems.at[len(copies)],
                )
            )
    for copy in copies:
        copy.start()
    for copy in copies:
        copy.wait()


def cut(sources, plan, shapes, gates=(), near=False, limit=58):
    gates = jax.tree.leaves(gates)
    args = [*sources, *gates]
    hbm = pl.BlockSpec(memory_space=pltpu.HBM)
    vmem = pl.BlockSpec(memory_space=pltpu.VMEM)
    anywhere = pl.BlockSpec(memory_space=pl.ANY)
    return pl.pallas_call(
        functools.partial(cut_kernel, plan, len(args)),
        in_specs=[vmem if near else hbm] * len(sources) + [anywhere] * len(gates),
        out_specs=[hbm if near else vmem] * len(shapes),
        out_shape=[jax.ShapeDtypeStruct(shape, BF16) for shape in shapes],
        scratch_shapes=[pltpu.SemaphoreType.DMA((sum(len(p) for p in plan),))],
        compiler_params=pltpu.CompilerParams(vmem_limit_bytes=limit << 20),
        cost_estimate=TINY,
        name="cut",
    )(*args)


def relay_kernel(own, two, *refs):
    up, down, sems = refs[-3:]
    me = lax.axis_index("ctx")

    def moves(act):
        for way, out in enumerate((up, down)):
            for source, chosen in ((own, me == 1 + way), (two, me != 1 + way)):

                @pl.when(chosen)
                def _():
                    act(pltpu.make_async_copy(source, out, sems.at[way]))

    moves(lambda c: c.start())
    moves(lambda c: c.wait())


def relay(own, two, gates):
    hbm = pl.BlockSpec(memory_space=pltpu.HBM)
    out = jax.ShapeDtypeStruct(own.shape, BF16)
    return pl.pallas_call(
        relay_kernel,
        in_specs=[hbm] * 2 + [pl.BlockSpec(memory_space=pl.ANY)] * len(gates),
        out_shape=(out, out),
        scratch_shapes=[pltpu.SemaphoreType.DMA((2,))],
        compiler_params=pltpu.CompilerParams(vmem_limit_bytes=4 << 20),
        cost_estimate=TINY,
        name="relay",
    )(own, two, *gates)


def sort_kernel(blocks_ref, places_ref, *refs):
    out_ref = refs[-1]
    heads = out_ref.shape[0]
    size = blocks_ref.shape[1]
    for j in range(0, places_ref.shape[0], 2):
        pair = jnp.concatenate(
            [blocks_ref[places_ref[j + i]].astype(F32) for i in range(2)], axis=0
        ).astype(BF16)
        rows = slice(j * size, (j + 2) * size)
        for h in range(heads):
            out_ref[h, rows, :HD] = pair[:, h * HD : (h + 1) * HD]
            out_ref[h, rows, HD:] = pair[:, (heads + h) * HD : (heads + h + 1) * HD]


def sort_blocks(blocks, places, gates):
    anywhere = pl.BlockSpec(memory_space=pl.ANY)
    count, size, _ = blocks.shape
    return pl.pallas_call(
        sort_kernel,
        in_specs=[pl.BlockSpec(memory_space=pltpu.VMEM), pl.BlockSpec(memory_space=pltpu.SMEM)]
        + [anywhere] * len(gates),
        out_shape=jax.ShapeDtypeStruct((KVH, places.shape[0] * size, 2 * HD), BF16),
        compiler_params=pltpu.CompilerParams(vmem_limit_bytes=4 << 20),
        cost_estimate=TINY,
        name="sort_blocks",
    )(blocks, places, *gates)


STEP = 2 * HD


def share(total, shards, own, sib, cols):
    rows = own.shape[0] // shards
    for z in range(shards):
        here = slice(z * rows, (z + 1) * rows)
        own[here, cols] = total[2 * z * rows : (2 * z + 1) * rows]
        sib[here, cols] = total[(2 * z + 1) * rows : (2 * z + 2) * rows]


def hold_kernel(*refs):
    pass


def hold(first, second, gates):
    anywhere = pl.BlockSpec(memory_space=pl.ANY)
    return pl.pallas_call(
        hold_kernel,
        in_specs=[anywhere] * (2 + len(gates)),
        out_specs=[anywhere] * 2,
        out_shape=[jax.ShapeDtypeStruct(first.shape, BF16)] * 2,
        input_output_aliases={0: 0, 1: 1},
        compiler_params=pltpu.CompilerParams(vmem_limit_bytes=2 << 20),
        cost_estimate=TINY,
        name="hold",
    )(first, second, *gates)


def load_rows_kernel(*refs):
    parts, out_ref, sems = refs[:5], refs[-2], refs[-1]
    me = lax.axis_index("ctx")
    rows = parts[0].shape[0]

    def copies(act):
        for k in range(4):
            start = pl.multiple_of(lax.bitwise_xor(me, k) * rows, rows)
            target = out_ref.at[pl.ds(start, rows)]
            if k < 3:
                act(pltpu.make_async_copy(parts[k], target, sems.at[k]))
            else:
                for source, chosen in ((parts[3], me >= 2), (parts[4], me < 2)):

                    @pl.when(chosen)
                    def _():
                        act(pltpu.make_async_copy(source, target, sems.at[k]))

    copies(lambda c: c.start())
    copies(lambda c: c.wait())


def load_rows(parts, gate):
    rows, width = parts[0].shape
    return pl.pallas_call(
        load_rows_kernel,
        in_specs=[pl.BlockSpec(memory_space=pltpu.HBM)] * 5 + [pl.BlockSpec(memory_space=pl.ANY)],
        out_shape=jax.ShapeDtypeStruct((4 * rows, width), BF16),
        scratch_shapes=[pltpu.SemaphoreType.DMA((4,))],
        compiler_params=pltpu.CompilerParams(vmem_limit_bytes=12 << 20),
        cost_estimate=TINY,
        name="load_rows",
    )(*parts, gate)


def load_weights_kernel(kv, q, first_x, first_y, last_x, last_y, out_ref, token, sems):
    depth = kv.shape[0]
    copies = []
    for r, sources in enumerate(((kv, q), (first_x, last_x), (first_y, last_y))):
        col = 0
        for source in sources:
            width = source.shape[1]
            target = out_ref.at[pl.ds(r * depth, depth), pl.ds(col, width)]
            copies.append(pltpu.make_async_copy(source, target, sems.at[len(copies)]))
            col += width
    for copy in copies:
        copy.start()
    token[...] = jnp.zeros(token.shape, F32)
    for copy in copies:
        copy.wait()


def load_weights(*parts):
    depth = parts[0].shape[0]
    cols = parts[0].shape[1] + parts[1].shape[1]
    return pl.pallas_call(
        load_weights_kernel,
        in_specs=[pl.BlockSpec(memory_space=pltpu.HBM)] * 6,
        out_shape=(
            jax.ShapeDtypeStruct((3 * depth, cols), BF16),
            jax.ShapeDtypeStruct((8, HD), F32),
        ),
        scratch_shapes=[pltpu.SemaphoreType.DMA((6,))],
        compiler_params=pltpu.CompilerParams(vmem_limit_bytes=16 << 20),
        cost_estimate=TINY,
        name="load_weights",
    )(*parts)


def gather_kernel(asked_ref, store_ref, *refs):
    out_ref, sems = refs[-2:]
    owners, cap = asked_ref.shape
    copies = [
        pltpu.make_async_copy(
            store_ref.at[asked_ref[i, j]], out_ref.at[i * cap + j], sems.at[i * cap + j]
        )
        for i in range(owners)
        for j in range(cap)
    ]
    for copy in copies:
        copy.start()
    for copy in copies:
        copy.wait()


def gather_blocks(asked, store_kv, gate):
    return pl.pallas_call(
        gather_kernel,
        in_specs=[
            pl.BlockSpec(memory_space=pltpu.SMEM),
            pl.BlockSpec(memory_space=pltpu.HBM),
            pl.BlockSpec(memory_space=pl.ANY),
        ],
        out_shape=jax.ShapeDtypeStruct((asked.size,) + store_kv.shape[1:], BF16),
        scratch_shapes=[pltpu.SemaphoreType.DMA((asked.size,))],
        compiler_params=pltpu.CompilerParams(vmem_limit_bytes=4 << 20),
        cost_estimate=TINY,
        name="gather_blocks",
    )(asked, store_kv, gate)


def diagonal_part(a_ref, d_x, d_y, col):
    h = d_x.shape[0]
    part = jnp.dot(a_ref[:, 6 * h : 7 * h], d_x[:, col : col + STEP], preferred_element_type=F32)
    return part + jnp.dot(a_ref[:, 7 * h :], d_y[:, col : col + STEP], preferred_element_type=F32)


def project_near_kernel(a_ref, w_ref, first, last):
    depth = w_ref.shape[0] // 3
    col = 0
    for out in (first, last):
        for here in range(0, out.shape[1], STEP):
            total = 0.0
            for r in range(3):
                part = slice(r * depth, (r + 1) * depth)
                total += jnp.dot(
                    a_ref[:, part], w_ref[part, col : col + STEP], preferred_element_type=F32
                )
            out[:, here : here + STEP] = total
            col += STEP


def project_first_kernel(a_ref, d_x, d_y, rest, kv_own, kv_sib, own, sib):
    for col in range(0, rest.shape[1], STEP):
        total = rest[:, col : col + STEP] + diagonal_part(a_ref, d_x, d_y, col)
        if col == 0:
            share(total, 4, kv_own, kv_sib, slice(0, STEP))
        else:
            share(total, 4, own, sib, slice(col - STEP, col))


def project_last_kernel(a_ref, d_x, d_y, rest, *refs):
    own, sib = refs[-2:]
    for col in range(0, rest.shape[1], STEP):
        total = rest[:, col : col + STEP] + diagonal_part(a_ref, d_x, d_y, col)
        share(total, 4, own, sib, slice(col, col + STEP))


def project(kernel, near, gates, outs, limit):
    vmem = pl.BlockSpec(memory_space=pltpu.VMEM)
    return pl.pallas_call(
        kernel,
        in_specs=[vmem] * len(near) + [pl.BlockSpec(memory_space=pl.ANY)] * len(gates),
        out_shape=[jax.ShapeDtypeStruct(shape, F32) for shape in outs],
        compiler_params=pltpu.CompilerParams(vmem_limit_bytes=limit << 20),
        cost_estimate=TINY,
        name="project",
    )(*near, *gates)


def fresh_kernel(own, sib, fresh_ref, first_ref, second_ref):
    me = lax.axis_index("ctx")
    fresh = own[...] + sib[...]
    low, high = fresh[:, :HD], fresh[:, HD:]
    fresh_ref[...] = fresh.astype(BF16)
    first_ref[...] = jnp.where(me == 0, high, low).astype(BF16)
    second_ref[...] = jnp.where(me == 3, low, high).astype(BF16)


def make_fresh(own, sib):
    rows = own.shape[0]
    out = lambda cols: jax.ShapeDtypeStruct((rows, cols), BF16)
    return pl.pallas_call(
        fresh_kernel,
        out_shape=(out(2 * HD), out(HD), out(HD)),
        compiler_params=pltpu.CompilerParams(vmem_limit_bytes=4 << 20),
        cost_estimate=TINY,
        name="fresh",
    )(own, sib)


def turn(values, cosine, sine):
    return values * cosine + pltpu.roll(values, HD // 2, 1) * sine


def assemble_kernel(fresh_ref, first_ref, second_ref, cached_ref, cos_ref, sin_ref, target_ref, key_ref, value_ref):
    me = lax.axis_index("ctx")
    low, high = fresh_ref[:, :HD].astype(F32), fresh_ref[:, HD:].astype(F32)
    first, second = first_ref[...].astype(F32), second_ref[...].astype(F32)
    fresh_key = jnp.where(me == 0, low, jnp.where(me == 3, second, first))
    fresh_value = jnp.where(me == 0, first, jnp.where(me == 3, high, second)).astype(BF16)
    fresh_key = turn(fresh_key, cos_ref[...], sin_ref[...]).astype(BF16)
    context = cached_ref.shape[0]
    count = fresh_key.shape[0]
    hit = lax.broadcasted_iota(jnp.int32, (context, count), 0) == target_ref[...]
    pick = jnp.where(hit, 1.0, 0.0)
    taken = jnp.max(pick, axis=1, keepdims=True) > 0.5
    pick = pick.astype(BF16)
    key_new = jnp.dot(pick, fresh_key, preferred_element_type=F32).astype(BF16)
    value_new = jnp.dot(pick, fresh_value, preferred_element_type=F32).astype(BF16)
    key_ref[...] = jnp.where(taken, key_new, cached_ref[:, :HD])
    value_ref[...] = jnp.where(taken, value_new, cached_ref[:, HD:]).T


def assemble(fresh, first, second, cached, cosine, sine, targets):
    context = cached.shape[0]
    return pl.pallas_call(
        assemble_kernel,
        out_shape=(
            jax.ShapeDtypeStruct((context, HD), BF16),
            jax.ShapeDtypeStruct((HD, context), BF16),
        ),
        compiler_params=pltpu.CompilerParams(vmem_limit_bytes=16 << 20),
        cost_estimate=TINY,
        name="assemble",
    )(fresh, first, second, cached, cosine, sine, targets)


def attend_kernel(heads, *refs):
    own_ref, sib_ref, key_ref, value_ref, cos_ref, sin_ref, pos_ref, key_pos_ref, *rest = refs
    out_ref = rest[-1]
    visible = key_pos_ref[...] <= pos_ref[...]
    for h in range(heads):
        cols = slice(h * HD, (h + 1) * HD)
        raw = own_ref[:, cols] + sib_ref[:, cols]
        query = (turn(raw, cos_ref[...], sin_ref[...]) * HD ** (-0.5)).astype(BF16)
        scores = lax.dot_general(
            key_ref[...], query, (((1,), (1,)), ((), ())), preferred_element_type=F32
        )
        scores = jnp.where(visible, scores, -1e30)
        exponent = jnp.exp(scores - jnp.max(scores, axis=0, keepdims=True))
        weights = exponent * (1.0 / jnp.sum(exponent, axis=0, keepdims=True))
        turned = jnp.dot(value_ref[...], weights.astype(BF16), preferred_element_type=F32)
        out_ref[:, cols] = turned.T.astype(BF16)


def attend(own, sib, shared, width, start, before):
    rec_count, cols = own.shape
    args = [own, sib, *shared]
    specs = [pl.BlockSpec(a.shape, lambda i: (0, 0)) for a in args]
    aliases = {}
    if before is not None:
        aliases = {len(args): 0}
        args.append(before)
        specs.append(pl.BlockSpec(memory_space=pltpu.HBM))
    return pl.pallas_call(
        functools.partial(attend_kernel, cols // HD),
        grid=(1,),
        in_specs=specs,
        out_specs=pl.BlockSpec((rec_count, cols), lambda i: (0, start // cols)),
        out_shape=jax.ShapeDtypeStruct((rec_count, width), BF16),
        input_output_aliases=aliases,
        compiler_params=pltpu.CompilerParams(vmem_limit_bytes=16 << 20),
        cost_estimate=TINY,
        name="attend",
    )(*args)


def fast_body(store_kv, block_slot, block_owner, rec_pos, states, w_query, w_keyval):
    store_count = lax.axis_size("store")
    ctx_count = lax.axis_size("ctx")
    my_index = lax.axis_index("ctx")
    piece_rows = store_kv.shape[1]
    block_count = block_slot.shape[1]
    rec_count = rec_pos.shape[1]
    query_cols = w_query.shape[1]
    depth = w_query.shape[0]
    positions = rec_pos[0]
    xf, yf, cf = (flip(b, store_count) for b in (XBIT, YBIT, CORE))
    by_x = lambda a: lax.ppermute(a, "store", xf)
    by_y = lambda a: lax.ppermute(a, "store", yf)
    by_core = lambda a: lax.ppermute(a, "store", cf)

    along = lambda a, pairs: lax.ppermute(a, "ctx", pairs)
    kv_cols = w_keyval.shape[1]
    late = query_cols // 2
    early = query_cols - late
    first_cols = kv_cols + early
    half = depth // 2

    asked, places = swap_ids(block_slot[0], block_owner[0], store_count)
    (w_first,) = cut(
        (w_keyval, w_query),
        [[(0, (0, 0), (0, 0), (depth, kv_cols)), (1, (0, 0), (0, kv_cols), (depth, early))]],
        [(depth, first_cols)],
    )
    first_x, first_y = by_x(w_first), by_y(w_first)
    gathered = gather_blocks(asked, store_kv, asked)
    arrived = lax.all_to_all(gathered, "store", split_axis=0, concat_axis=0, tiled=True)
    (w_last,) = cut(
        (w_query,), [[(0, (0, early), (0, 0), (depth, late))]], [(depth, late)], (arrived, first_x, first_y), limit=8
    )
    last_x, last_y = by_x(w_last), by_y(w_last)
    by_head = sort_blocks(arrived, places, (w_last,))
    cached = lax.all_to_all(by_head, "ctx", split_axis=0, concat_axis=0, tiled=True)
    cached = cached.reshape(-1, 2 * HD)

    keep, send = norm_split(states[0])
    shard, width = keep.shape
    (both,) = cut(
        (keep, by_core(send)),
        [[(0, (0, 0), (0, 0), (shard, width)), (1, (0, 0), (shard, 0), (shard, width))]],
        [(2 * shard, width)],
        near=True,
        limit=4,
    )
    along = lambda a, pairs: lax.ppermute(a, "ctx", pairs)
    two = along(both, [(0, 2), (1, 3), (2, 0), (3, 1)])
    one = along(both, [(0, 1), (1, 0), (2, 3), (3, 2)])
    up, down = relay(both, two, (one,))
    shard_parts = (
        both,
        one,
        two,
        along(up, [(1, 2), (2, 3)]),
        along(down, [(2, 1), (1, 0)]),
    )

    def diagonal(from_x, from_y, gates, limit, late_gates=()):
        cols = from_x.shape[1]
        sent = cut(
            (from_y, from_x),
            [[(0, (0, 0), (0, 0), (half, cols))], [(1, (half, 0), (0, 0), (half, cols))]],
            [(half, cols)] * 2,
            gates,
            limit=limit,
        )
        if late_gates:
            sent = hold(*sent, late_gates)
        return (by_x(sent[0]), by_y(sent[1])), sent[0]

    diag_first, _ = diagonal(first_x, first_y, (up, cached), 8, (last_x, last_y))
    weights, loaded = load_weights(w_keyval, w_query, first_x, first_y, last_x, last_y)
    diag_last, sent_last = diagonal(last_x, last_y, (loaded,), 6)

    shard_rows = block_count * piece_rows
    frequency = jnp.exp(
        jnp.arange(HD // 2, dtype=F32) * (-2.0 * math.log(500000.0) / HD)
    )
    angles = positions.astype(F32)[:, None] * frequency[None, :]
    cos_half, sin_half = jnp.cos(angles), jnp.sin(angles)
    cosine = jnp.concatenate((cos_half, cos_half), axis=1)
    sine = jnp.concatenate((-sin_half, sin_half), axis=1)
    block_len = piece_rows * ctx_count
    targets = (
        positions % block_len // piece_rows * shard_rows
        + positions // block_len * piece_rows
        + positions % piece_rows
    )

    row_ids = jnp.arange(ctx_count * shard_rows)
    key_pos = (
        row_ids % shard_rows // piece_rows * block_len
        + row_ids // shard_rows * piece_rows
        + row_ids % piece_rows
    )

    rows = load_rows(shard_parts, sent_last)
    first_part, last_part = project(
        project_near_kernel,
        (rows, weights),
        (),
        [(2 * rec_count, first_cols), (2 * rec_count, late)],
        20,
    )
    kv_own, kv_sib, early_own, early_sib = project(
        project_first_kernel,
        (rows, *diag_first, first_part),
        (),
        [(rec_count, kv_cols)] * 2 + [(rec_count, early)] * 2,
        14,
    )
    fresh, to_first, to_second = make_fresh(kv_own, by_core(kv_sib))
    first = along(to_first, [(0, 1), (1, 2), (2, 0)])
    second = along(to_second, [(1, 3), (2, 1), (3, 2)])
    key_rows, value_rows = assemble(
        fresh, first, second, cached, cosine, sine, targets.reshape(1, rec_count)
    )
    shared = (
        key_rows,
        value_rows,
        cosine,
        sine,
        positions.reshape(1, rec_count),
        key_pos.reshape(-1, 1),
    )
    result = attend(early_own, by_core(early_sib), shared, query_cols, 0, None)
    own, sib = project(
        project_last_kernel,
        (rows, *diag_last, last_part),
        (first, second, cached),
        [(rec_count, late)] * 2,
        12,
    )
    result = attend(own, by_core(sib), shared, query_cols, early, result)
    return result.reshape(1, rec_count, query_cols)


def solution(mesh):
    fast = mesh.shape["store"] == 8 and mesh.shape["ctx"] == KVH
    return jax.shard_map(
        fast_body if fast else general_body,
        mesh=mesh,
        in_specs=(
            P("store", "ctx", None),
            P("store", None),
            P("store", None),
            P("store", None),
            P("store", "ctx", None),
            P("store", "ctx"),
            P("store", "ctx"),
        ),
        out_specs=P("store", None, "ctx"),
        check_vma=False,
    )
```
